1024 devices in a mesh: bx: 64 (over x, y, core), by: 16 (over z).
Axes of the slice: x: 4, y: 8, z: 16, core: 2. Of those that a mesh axis runs over, the one named last changes fastest.
Arguments:
- pops_old: float32 [6144, 19, 512], P(('bx', 'by')), as said below
- old_owner: int32 [2048], replicated, may hold values from 0 to 1023, as said below
- relax: float32 [2048], P(('bx', 'by')), may hold values from 0.6 to 1.8
- solid_mask: int32 [2048, 512], P(('bx', 'by')), may hold values 0 or 1
Outputs:
- populations: float32 [2048, 19, 512], P(('bx', 'by'))
The draws below stay inside these ranges and needn't reach their ends.
Inputs may be any that keep to these rules, and one draw needn't show every extreme that they name: `old_owner`: block b's new owner is device b // 2 (index bx * 16 + by). Its old owner's bx index differs from the new one's by at most one, without wrap; among the blocks of one block column gx and one gz, the old owners' by indices are the new ones' shifted cyclically by an amount that differs between the gz of that column. One device holds at most 6 blocks before the rebalance and some device holds exactly 6. `pops_old`: row d * 6 + k holds the k-th block, in increasing block number, whose old owner is device d; rows past a device's count of blocks are unused.
All inputs are finite; a program needn't handle non-finite values. No bound on the sum of `solid_mask` on one device may be relied on, other than what follows from the above.
Results may differ from the reference program's by a relative error of at most 0.0003.
Values sent between devices are 32-bit elements; how exact they have to be, the bound alone decides.
No kernel may reach another device: no remote copies, remote signals or barrier semaphores. Data moves between devices by JAX's collectives and lax.ppermute only.
A program may use at most 64 MiB of HBM per device.

```python
import math
import jax
import jax.numpy as jnp
import numpy as np
from jax import lax

BL = 8
TZ = 2
MOST = 6
CELLS = 512
BLOCKS = 2048
SLOTS = 6144
N_BX = 64
N_BY = 16
DEVICES = 1024


WEIGHTS = np.array([1.0 / 3.0] + [1.0 / 18.0] * 6 + [1.0 / 36.0] * 12)


def draw_old_owner(key, part):
    key = jax.random.fold_in(key, 11)
    first, second, third = jax.random.split(key, 3)
    column = jnp.arange(N_BX, dtype=jnp.int32)[:, None]
    offset = jax.random.randint(first, (N_BX, TZ), -1, 2).astype(jnp.int32)
    offset = jnp.where((column + offset < 0) | (column + offset >= N_BX), 0, offset)
    centre = jax.random.randint(second, (), 1, N_BX - 1).astype(jnp.int32)
    offset = jnp.where(column == centre - 1, 1, jnp.where(column == centre, 0, jnp.where(column == centre + 1, -1, offset)))
    subkeys = jax.random.split(third, N_BX)
    shifts = jax.vmap(lambda subkey: jax.random.permutation(subkey, N_BY))(subkeys)[:, :TZ].astype(jnp.int32)
    rows = jnp.arange(N_BY, dtype=jnp.int32)[None, :, None]
    owner_x = (column + offset)[:, None, :]
    owner_y = (rows + shifts[:, None, :]) % N_BY
    return (owner_x * N_BY + owner_y).reshape(-1).astype(jnp.int32)


def draw_pops_old(key, part):
    key = jax.random.fold_in(key, 23)
    first, second = jax.random.split(key)
    weight = jnp.asarray(WEIGHTS, jnp.float32).reshape(1, 19, 1)
    noise = jnp.clip(jax.random.normal(first, (SLOTS, 19, CELLS), jnp.float32), -3.0, 3.0)
    values = weight * (1.0 + 0.25 * noise)
    return values.astype(jnp.float32)


def touch_ends(entries, own_key, smallest, high):
    longest = entries.shape.index(max(entries.shape))
    spots = []
    for shift in (0, 1):
        where = [jax.random.randint(jax.random.fold_in(own_key, axis), (), 0, length) for axis, length in enumerate(entries.shape)]
        where[longest] = (where[longest] + shift) % entries.shape[longest]
        spots.append(tuple(where))
    return entries.at[spots[0]].set(smallest).at[spots[1]].set(high)


def shard_levels(rng, dims, shards, smallest, largest):
    def one(axis_at, shards_of):
        draws = jax.random.uniform(jax.random.fold_in(jax.random.fold_in(rng, 6), axis_at), (shards_of,), jnp.float32, smallest / len(shards), largest / len(shards))
        return jnp.repeat(jnp.exp(draws), dims[axis_at] // shards_of).reshape((-1,) + (1,) * (len(dims) - axis_at - 1))

    level = one(*shards[0])
    for cut in shards[1:]:
        level = level * one(*cut)
    return level


def setup_inputs(seed: int = 0) -> dict:
    key_list = jax.random.split(jax.random.key(seed), 5)
    return {
        "pops_old": draw_pops_old(jax.random.fold_in(key_list[4], 71), 0),
        "old_owner": draw_old_owner(jax.random.fold_in(key_list[4], 71), 0),
        "relax": jnp.clip(jnp.exp(math.log(1.8) - 1.0986122 * jax.random.uniform(key_list[2], (BLOCKS,), jnp.float32) ** shard_levels(key_list[2], (BLOCKS,), ((0, 1024),), -0.2, 0.2)), 0.6, 1.8),
        "solid_mask": touch_ends((jax.random.randint(key_list[3], (BLOCKS, CELLS), 0, 10) < 3).astype(jnp.int32), jax.random.fold_in(key_list[3], 1), 0, 1),
    }


VELOCITY = np.array([[0, 0, 0], [1, 0, 0], [-1, 0, 0], [0, 1, 0], [0, -1, 0], [0, 0, 1], [0, 0, -1],
                     [1, 1, 0], [-1, -1, 0], [1, -1, 0], [-1, 1, 0], [1, 0, 1], [-1, 0, -1], [1, 0, -1],
                     [-1, 0, 1], [0, 1, 1], [0, -1, -1], [0, 1, -1], [0, -1, 1]])
OPPOSITE = np.array([0, 2, 1, 4, 3, 6, 5, 8, 7, 10, 9, 12, 11, 14, 13, 16, 15, 18, 17])
WEIGHTS = np.array([1.0 / 3.0] + [1.0 / 18.0] * 6 + [1.0 / 36.0] * 12)
MAGIC_TRT = 0.1875


def collide(pop_field, omega_plus, solid_flag):
    tail = (19,) + (1,) * (pop_field.ndim - 1)
    vel_x = jnp.asarray(VELOCITY[:, 0], jnp.float32).reshape(tail)
    vel_y = jnp.asarray(VELOCITY[:, 1], jnp.float32).reshape(tail)
    vel_z = jnp.asarray(VELOCITY[:, 2], jnp.float32).reshape(tail)
    weight = jnp.asarray(WEIGHTS, jnp.float32).reshape(tail)
    density = jnp.sum(pop_field, axis=0)
    flux_x = jnp.sum(pop_field * vel_x, axis=0)
    flux_y = jnp.sum(pop_field * vel_y, axis=0)
    flux_z = jnp.sum(pop_field * vel_z, axis=0)
    projection = vel_x * flux_x + vel_y * flux_y + vel_z * flux_z
    square = flux_x * flux_x + flux_y * flux_y + flux_z * flux_z
    even_eq = weight * (density + 4.5 * projection * projection - 1.5 * square)
    odd_eq = weight * 3.0 * projection
    mirror = pop_field[OPPOSITE]
    even_part = 0.5 * (pop_field + mirror)
    odd_part = 0.5 * (pop_field - mirror)
    omega_minus = 1.0 / (MAGIC_TRT / (1.0 / omega_plus - 0.5) + 0.5)
    relaxed = pop_field - omega_plus * (even_part - even_eq) - omega_minus * (odd_part - odd_eq)
    return jnp.where(solid_flag, mirror, relaxed)


def collide_blocks(blocks, relax, solid_mask):
    group = N_BY * TZ
    grouped = blocks.reshape(N_BX, group, 19, CELLS)
    rates = relax.reshape(N_BX, group)
    flags = solid_mask.reshape(N_BX, group, CELLS)

    def one_group(pieces):
        block_set, rate_set, flag_set = pieces
        moved = jnp.transpose(block_set, (1, 0, 2))
        result = collide(moved, rate_set[:, None], flag_set == 1)
        return jnp.transpose(result, (1, 0, 2))

    return lax.map(one_group, (grouped, rates, flags)).reshape(BLOCKS, 19, CELLS)


def to_field(blocks):
    shaped = blocks.reshape(N_BX, N_BY, TZ, 19, BL, BL, BL)
    shaped = jnp.transpose(shaped, (3, 0, 4, 1, 5, 2, 6))
    return shaped.reshape(19, N_BX * BL, N_BY * BL, TZ * BL)


def from_field(pop_field):
    shaped = pop_field.reshape(19, N_BX, BL, N_BY, BL, TZ, BL)
    shaped = jnp.transpose(shaped, (1, 3, 5, 0, 2, 4, 6))
    return shaped.reshape(BLOCKS, 19, CELLS)


def reference(pops_old, old_owner, relax, solid_mask):
    counts = jnp.zeros((DEVICES,), jnp.int32).at[old_owner].add(1)
    starts = jnp.cumsum(counts) - counts
    order = jnp.argsort(old_owner, stable=True).astype(jnp.int32)
    position = jnp.zeros((BLOCKS,), jnp.int32).at[order].set(jnp.arange(BLOCKS, dtype=jnp.int32))
    ranking = position - starts[old_owner]
    source = (old_owner * MOST + ranking).astype(jnp.int32)
    blocks = jnp.take(pops_old, source, axis=0)
    for repeat in range(2):
        relaxed = collide_blocks(blocks, relax, solid_mask)
        lattice = to_field(relaxed)
        read = jnp.stack([jnp.roll(lattice[number], (int(VELOCITY[number, 0]), int(VELOCITY[number, 1]), int(VELOCITY[number, 2])), axis=(0, 1, 2)) for number in range(19)])
        blocks = from_field(read)
    return blocks
```

```python
import functools

import jax
import jax.numpy as jnp
import numpy as np
from jax import lax
from jax.experimental import pallas as pl
from jax.experimental.pallas import tpu as pltpu
from jax.sharding import PartitionSpec as P

EDGE = 8
POPS = 19
TILES = 4
LANES = 128
ROWS = POPS * TILES
CHANNELS = POPS + 2
SOLID = POPS
RATE = POPS + 1
SPAN = 16
GROUPS = (CHANNELS + 3) // 4

VELOCITY = (
    (0, 0, 0), (1, 0, 0), (-1, 0, 0), (0, 1, 0), (0, -1, 0), (0, 0, 1), (0, 0, -1),
    (1, 1, 0), (-1, -1, 0), (1, -1, 0), (-1, 1, 0), (1, 0, 1), (-1, 0, -1), (1, 0, -1),
    (-1, 0, 1), (0, 1, 1), (0, -1, -1), (0, 1, -1), (0, -1, 1),
)
WEIGHTS = (1.0 / 3.0,) + (1.0 / 18.0,) * 6 + (1.0 / 36.0,) * 12
MAGIC_TRT = 0.1875

VMEM = pl.BlockSpec(memory_space=pltpu.VMEM)
SMEM = pl.BlockSpec(memory_space=pltpu.SMEM)


def roll(value, shift, axis):
    size = value.shape[axis]
    shift = shift % size
    return value if shift == 0 else pltpu.roll(value, shift, axis)


def lane_of(shape):
    return lax.broadcasted_iota(jnp.int32, shape, len(shape) - 1)


def pair_index(low, high, count):
    return low * (2 * count - low - 1) // 2 + (high - low - 1)


def collide(pops, rate, solid):
    rho = functools.reduce(jnp.add, pops)
    flux = []
    for axis in range(3):
        plus = functools.reduce(jnp.add, [pops[q] for q in range(POPS) if VELOCITY[q][axis] > 0])
        minus = functools.reduce(jnp.add, [pops[q] for q in range(POPS) if VELOCITY[q][axis] < 0])
        flux.append(plus - minus)
    base = rho - 1.5 * (flux[0] * flux[0] + flux[1] * flux[1] + flux[2] * flux[2])
    rate_odd = 1.0 / (MAGIC_TRT / (1.0 / rate - 0.5) + 0.5)
    relaxed = [None] * POPS
    rest = pops[0] - rate * (pops[0] - WEIGHTS[0] * base)
    relaxed[0] = jnp.where(solid, pops[0], rest)
    for q in range(1, POPS, 2):
        one, two = pops[q], pops[q + 1]
        speed = None
        for axis in range(3):
            if VELOCITY[q][axis] != 0:
                term = flux[axis] if VELOCITY[q][axis] > 0 else -flux[axis]
                speed = term if speed is None else speed + term
        even = rate * (0.5 * (one + two) - WEIGHTS[q] * (base + 4.5 * speed * speed))
        odd = rate_odd * (0.5 * (one - two) - (3.0 * WEIGHTS[q]) * speed)
        relaxed[q] = jnp.where(solid, two, one - even - odd)
        relaxed[q + 1] = jnp.where(solid, one, two - even + odd)
    return relaxed


def gather_kernel(count_x, count_y, depth, where_ref, owner_ref, pops_ref, one_ref, two_ref, keep_ref, meta_ref):
    my_x, my_y = where_ref[0], where_ref[1]
    myself = my_x * count_y + my_y
    odd = lax.rem(my_x, 2)
    found, level = {}, {}
    for offset in (-1, 0, 1):
        place = my_x + offset
        inside = (place >= 0) & (place < count_x)
        start = jnp.clip(place, 0, count_x - 1) * (count_y * depth)
        for layer in range(depth):
            shift = lax.rem(owner_ref[start + layer], count_y)
            row = lax.rem(my_y - shift + count_y, count_y)
            hit = (owner_ref[start + row * depth + layer] == myself) & inside
            found[offset, layer] = hit.astype(jnp.int32)
            level[offset, layer] = row * depth + layer
    slots = {}
    before = jnp.int32(0)
    for offset in (-1, 0, 1):
        for layer in range(depth):
            slot = before
            for other in range(depth):
                if other != layer:
                    slot = slot + found[offset, other] * (level[offset, other] < level[offset, layer]).astype(jnp.int32)
            slots[offset, layer] = jnp.minimum(slot, pops_ref.shape[0] - 1)
        for layer in range(depth):
            before = before + found[offset, layer]
    start = my_x * (count_y * depth)
    shift0 = lax.rem(owner_ref[start], count_y)
    shift1 = lax.rem(owner_ref[start + 1], count_y)
    low, high = jnp.minimum(shift0, shift1), jnp.maximum(shift0, shift1)
    meta_ref[0] = pair_index(low, high, count_y)
    meta_ref[1] = (shift0 > shift1).astype(jnp.int32)
    meta_ref[2] = odd
    for layer, shift in ((0, shift0), (1, shift1)):
        row = lax.rem(my_y - shift + count_y, count_y)
        source = owner_ref[start + row * depth + layer] // count_y - my_x
        meta_ref[3 + layer] = jnp.where(source == 0, 0, jnp.where(source == 1 - 2 * odd, 1, 2))
    for layer in range(depth):
        left, right = slots[-1, layer], slots[1, layer]
        one = jnp.where(odd == 1, left, right)
        two = jnp.where(odd == 1, right, left)
        for ref, slot in ((one_ref, one), (two_ref, two), (keep_ref, slots[0, layer])):
            for tile in range(TILES):
                ref[pl.ds(layer * ROWS + tile * POPS, POPS), :] = pops_ref[slot, :, tile * LANES:(tile + 1) * LANES]


def select_kernel(meta_ref, one_ref, two_ref, keep_ref, low_ref, high_ref):
    swapped = meta_ref[1] == 1
    blocks = []
    for layer in range(2):
        source = meta_ref[3 + layer]
        part = pl.ds(layer * ROWS, ROWS)
        blocks.append(
            jnp.where(source == 0, keep_ref[part, :], jnp.where(source == 1, one_ref[part, :], two_ref[part, :]))
        )
    low_ref[...] = jnp.where(swapped, blocks[1], blocks[0])
    high_ref[...] = jnp.where(swapped, blocks[0], blocks[1])


def collide_kernel(meta_ref, rate_ref, solid_ref, low_ref, high_ref, state_ref, one_ref, two_ref):
    swapped = meta_ref[1] == 1
    odd = meta_ref[2] == 1
    wide = lane_of((POPS, LANES)) < 64
    for tile in range(TILES):
        part = pl.ds(tile * POPS, POPS)
        low, high = low_ref[part, :], high_ref[part, :]
        lower = jnp.where(swapped, high, low)
        upper = jnp.where(swapped, low, high)
        state_ref[pl.ds(2 * tile, POPS, stride=EDGE), :] = jnp.where(wide, lower, roll(upper, 64, 1))
        state_ref[pl.ds(2 * tile + 1, POPS, stride=EDGE), :] = jnp.where(wide, roll(lower, 64, 1), upper)
    narrow = lane_of((1, LANES)) < 64
    for tile in range(TILES):
        flags = jnp.where(solid_ref[:, tile * LANES:(tile + 1) * LANES] == 1, 1.0, 0.0)
        lower, upper = flags[0:1, :], flags[1:2, :]
        row = SOLID * EDGE + 2 * tile
        state_ref[pl.ds(row, 1), :] = jnp.where(narrow, lower, roll(upper, 64, 1))
        state_ref[pl.ds(row + 1, 1), :] = jnp.where(narrow, roll(lower, 64, 1), upper)
    rate = jnp.where(lane_of((EDGE, LANES)) < 64, rate_ref[0], rate_ref[1])
    state_ref[pl.ds(RATE * EDGE, EDGE), :] = rate
    solid = state_ref[pl.ds(SOLID * EDGE, EDGE), :] > 0.5
    pops = [state_ref[pl.ds(q * EDGE, EDGE), :] for q in range(POPS)]
    for q, value in enumerate(collide(pops, rate, solid)):
        state_ref[pl.ds(q * EDGE, EDGE), :] = value
    for count, place, mine, theirs in ((CHANNELS, 0, EDGE - 1, 0), (POPS, CHANNELS, EDGE - 2, 1)):
        right = state_ref[pl.ds(mine, count, stride=EDGE), :]
        left = state_ref[pl.ds(theirs, count, stride=EDGE), :]
        one_ref[pl.ds(place, count), :] = jnp.where(odd, left, right)
        two_ref[pl.ds(place, count), :] = jnp.where(odd, right, left)


def extend(meta_ref, state_ref, one_ref, two_ref, wide_ref):
    odd = meta_ref[2] == 1
    for channel in range(CHANNELS):
        wide_ref[pl.ds(channel * SPAN + 4, EDGE), :] = state_ref[pl.ds(channel * EDGE, EDGE), :]
    for count, place, low, high in ((CHANNELS, 0, 3, 12), (POPS, CHANNELS, 2, 13)):
        one, two = one_ref[pl.ds(place, count), :], two_ref[pl.ds(place, count), :]
        wide_ref[pl.ds(low, count, stride=SPAN), :] = jnp.where(odd, one, two)
        wide_ref[pl.ds(high, count, stride=SPAN), :] = jnp.where(odd, two, one)


def pack_kernel(meta_ref, state_ref, one_ref, two_ref, down_ref, up_ref, wide_ref):
    extend(meta_ref, state_ref, one_ref, two_ref, wide_ref)
    part = lane_of((SPAN, LANES)) // 16
    for ref, first in ((down_ref, 0), (up_ref, 48)):
        for group in range(GROUPS):
            packed = None
            for k in range(4):
                channel = group * 4 + k
                if channel >= CHANNELS:
                    continue
                value = wide_ref[pl.ds(channel * SPAN, SPAN), :]
                for layer in range(2):
                    moved = roll(value, k * 32 + layer * 16 - (layer * 64 + first), 1)
                    packed = moved if packed is None else jnp.where(part == 2 * k + layer, moved, packed)
            ref[pl.ds(group * SPAN, SPAN), :] = packed


def stream(fields, depth_place):
    moved = [[None] * POPS for _ in fields]
    for q in range(POPS):
        step_x, step_y, step_z = VELOCITY[q]
        for layer in range(2):
            value = roll(fields[layer][q], 8 * step_y + step_z, 1)
            if step_z != 0:
                outer = roll(fields[1 - layer][q], 8 * step_y - 7 * step_z, 1)
                value = jnp.where(depth_place == (0 if step_z > 0 else 7), outer, value)
            moved[layer][q] = roll(value, step_x, 0)
    return moved


def finish_kernel(meta_ref, state_ref, one_ref, two_ref, below_ref, above_ref, out_ref, wide_ref, last_ref):
    extend(meta_ref, state_ref, one_ref, two_ref, wide_ref)
    lane = lane_of((SPAN, LANES))
    place = lane % 8
    at_low = (lane >= 16) & (lane < 32)
    at_high = (lane >= 96) & (lane < 112)
    fields = [[None] * CHANNELS for _ in range(2)]
    for channel in range(CHANNELS):
        group, k = divmod(channel, 4)
        value = wide_ref[pl.ds(channel * SPAN, SPAN), :]
        below = below_ref[pl.ds(group * SPAN, SPAN), :]
        above = above_ref[pl.ds(group * SPAN, SPAN), :]
        for layer in range(2):
            at = k * 32 + layer * 16
            field = roll(value, 32 - 64 * layer, 1)
            field = jnp.where(at_low, roll(below, 16 - at, 1), field)
            fields[layer][channel] = jnp.where(at_high, roll(above, 96 - at, 1), field)
    moved = stream([field[:POPS] for field in fields], place)
    relaxed = [collide(moved[layer], fields[layer][RATE], fields[layer][SOLID] > 0.5) for layer in range(2)]
    final = stream(relaxed, place)
    half = lane_of((POPS, LANES)) < 64
    for layer in range(2):
        for q in range(POPS):
            last_ref[layer, pl.ds(q * SPAN, SPAN), :] = final[layer][q]
        for tile in range(TILES):
            even = last_ref[layer, pl.ds(2 * tile + 4, POPS, stride=SPAN), :]
            odd = last_ref[layer, pl.ds(2 * tile + 5, POPS, stride=SPAN), :]
            out_ref[layer, :, tile * LANES:(tile + 1) * LANES] = jnp.where(half, roll(even, -32, 1), roll(odd, 32, 1))


def shape_of(*dims, dtype=jnp.float32):
    return jax.ShapeDtypeStruct(dims, dtype)


def local(pops_old, old_owner, relax, solid_mask):
    count_x, count_y = lax.axis_size("bx"), lax.axis_size("by")
    depth = relax.shape[0]
    inside = [pair for k in range(0, count_x, 2) for pair in ((k, k + 1), (k + 1, k))]
    across = [
        pair for k in range(1, count_x, 2) for pair in ((k, (k + 1) % count_x), ((k + 1) % count_x, k))
    ]
    up = [(k, (k + 1) % count_y) for k in range(count_y)]
    down = [(k, (k - 1) % count_y) for k in range(count_y)]

    where = jnp.stack([lax.axis_index("bx"), lax.axis_index("by")]).astype(jnp.int32)
    one, two, keep, meta = pl.pallas_call(
        functools.partial(gather_kernel, count_x, count_y, depth),
        out_shape=[shape_of(depth * ROWS, LANES)] * 3 + [shape_of(8, dtype=jnp.int32)],
        in_specs=[SMEM, SMEM, VMEM],
        out_specs=[VMEM, VMEM, VMEM, SMEM],
        name="gather_blocks",
    )(where, old_owner, pops_old)
    two = lax.ppermute(two, "bx", across)
    one = lax.ppermute(one, "bx", inside)
    low, high = pl.pallas_call(
        select_kernel,
        out_shape=[shape_of(ROWS, LANES)] * 2,
        in_specs=[SMEM, VMEM, VMEM, VMEM],
        out_specs=[VMEM, VMEM],
        name="select_blocks",
    )(meta, one, two, keep)

    def shifted(block, shift):
        if shift == 0:
            return block
        return lax.ppermute(block, "by", [((k + shift) % count_y, k) for k in range(count_y)])

    def branch(first, second):
        return lambda a, b: (shifted(a, first), shifted(b, second))

    pairs = [(first, second) for first in range(count_y) for second in range(first + 1, count_y)]
    low, high = lax.switch(meta[0], [branch(*pair) for pair in pairs], low, high)

    state, one, two = pl.pallas_call(
        collide_kernel,
        out_shape=[shape_of(CHANNELS * EDGE, LANES)] + [shape_of(CHANNELS + POPS, LANES)] * 2,
        in_specs=[SMEM, SMEM, VMEM, VMEM, VMEM],
        out_specs=[VMEM] * 3,
        name="collide_first",
    )(meta, relax, solid_mask, low, high)
    two = lax.ppermute(two, "bx", across)
    one = lax.ppermute(one, "bx", inside)
    to_below, to_above = pl.pallas_call(
        pack_kernel,
        out_shape=[shape_of(GROUPS * SPAN, LANES)] * 2,
        in_specs=[SMEM, VMEM, VMEM, VMEM],
        out_specs=[VMEM] * 2,
        scratch_shapes=[pltpu.VMEM((CHANNELS * SPAN, LANES), jnp.float32)],
        name="pack_faces",
    )(meta, state, one, two)
    below = lax.ppermute(to_above, "by", up)
    above = lax.ppermute(to_below, "by", down)
    return pl.pallas_call(
        finish_kernel,
        out_shape=shape_of(depth, POPS, TILES * LANES),
        in_specs=[SMEM] + [VMEM] * 5,
        out_specs=VMEM,
        scratch_shapes=[
            pltpu.VMEM((CHANNELS * SPAN, LANES), jnp.float32),
            pltpu.VMEM((2, POPS * SPAN, LANES), jnp.float32),
        ],
        name="stream_collide_stream",
    )(meta, state, one, two, below, above)


def solution(mesh):
    return jax.shard_map(
        local,
        mesh=mesh,
        in_specs=(P(("bx", "by"), None, None), P(), P(("bx", "by")), P(("bx", "by"), None)),
        out_specs=P(("bx", "by"), None, None),
        check_vma=False,
    )
```

```python
import functools

import jax
import jax.numpy as jnp
import numpy as np
from jax import lax
from jax.experimental import pallas as pl
from jax.experimental.pallas import tpu as pltpu
from jax.sharding import PartitionSpec as P

EDGE = 8
POPS = 19
TILES = 4
LANES = 128
ROWS = POPS * TILES
CHANNELS = POPS + 2
SOLID = POPS
RATE = POPS + 1
SPAN = 16
GROUPS = (CHANNELS + 3) // 4

VELOCITY = (
    (0, 0, 0), (1, 0, 0), (-1, 0, 0), (0, 1, 0), (0, -1, 0), (0, 0, 1), (0, 0, -1),
    (1, 1, 0), (-1, -1, 0), (1, -1, 0), (-1, 1, 0), (1, 0, 1), (-1, 0, -1), (1, 0, -1),
    (-1, 0, 1), (0, 1, 1), (0, -1, -1), (0, 1, -1), (0, -1, 1),
)
WEIGHTS = (1.0 / 3.0,) + (1.0 / 18.0,) * 6 + (1.0 / 36.0,) * 12
MAGIC_TRT = 0.1875

VMEM = pl.BlockSpec(memory_space=pltpu.VMEM)
SMEM = pl.BlockSpec(memory_space=pltpu.SMEM)
HBM = pl.BlockSpec(memory_space=pltpu.HBM)
SMALL = pltpu.CompilerParams(vmem_limit_bytes=4 * 1024 * 1024)


def roll(value, shift, axis):
    size = value.shape[axis]
    shift = shift % size
    return value if shift == 0 else pltpu.roll(value, shift, axis)


def lane_of(shape):
    return lax.broadcasted_iota(jnp.int32, shape, len(shape) - 1)


def pair_index(low, high, count):
    return low * (2 * count - low - 1) // 2 + (high - low - 1)


def collide(pops, rate, solid):
    rho = functools.reduce(jnp.add, pops)
    flux = []
    for axis in range(3):
        plus = functools.reduce(jnp.add, [pops[q] for q in range(POPS) if VELOCITY[q][axis] > 0])
        minus = functools.reduce(jnp.add, [pops[q] for q in range(POPS) if VELOCITY[q][axis] < 0])
        flux.append(plus - minus)
    base = rho - 1.5 * (flux[0] * flux[0] + flux[1] * flux[1] + flux[2] * flux[2])
    rate_odd = 1.0 / (MAGIC_TRT / (1.0 / rate - 0.5) + 0.5)
    relaxed = [None] * POPS
    rest = pops[0] - rate * (pops[0] - WEIGHTS[0] * base)
    relaxed[0] = jnp.where(solid, pops[0], rest)
    for q in range(1, POPS, 2):
        one, two = pops[q], pops[q + 1]
        speed = None
        for axis in range(3):
            if VELOCITY[q][axis] != 0:
                term = flux[axis] if VELOCITY[q][axis] > 0 else -flux[axis]
                speed = term if speed is None else speed + term
        even = rate * (0.5 * (one + two) - WEIGHTS[q] * (base + 4.5 * speed * speed))
        odd = rate_odd * (0.5 * (one - two) - (3.0 * WEIGHTS[q]) * speed)
        relaxed[q] = jnp.where(solid, two, one - even - odd)
        relaxed[q + 1] = jnp.where(solid, one, two - even + odd)
    return relaxed


def gather_kernel(
    count_x, count_y, depth, owner_in, pops_in, rate_in, solid_in,
    one_ref, two_ref, extra_ref, meta_ref,
    owner_ref, pops_ref, rate_ref, solid_ref, sems,
):
    owner_copy = pltpu.make_async_copy(owner_in, owner_ref, sems.at[0])
    pops_copy = pltpu.make_async_copy(pops_in, pops_ref, sems.at[1])
    rate_copy = pltpu.make_async_copy(rate_in, rate_ref, sems.at[2])
    solid_copy = pltpu.make_async_copy(solid_in, solid_ref, sems.at[3])
    owner_copy.start()
    pops_copy.start()
    rate_copy.start()
    solid_copy.start()
    owner_copy.wait()
    my_x, my_y = lax.axis_index("bx"), lax.axis_index("by")
    myself = my_x * count_y + my_y
    odd = lax.rem(my_x, 2)
    found, level = {}, {}
    for offset in (-1, 0, 1):
        place = my_x + offset
        inside = (place >= 0) & (place < count_x)
        start = jnp.clip(place, 0, count_x - 1) * (count_y * depth)
        for layer in range(depth):
            shift = lax.rem(owner_ref[start + layer], count_y)
            row = lax.rem(my_y - shift + count_y, count_y)
            hit = (owner_ref[start + row * depth + layer] == myself) & inside
            found[offset, layer] = hit.astype(jnp.int32)
            level[offset, layer] = row * depth + layer
    slots = {}
    before = jnp.int32(0)
    for offset in (-1, 0, 1):
        for layer in range(depth):
            slot = before
            for other in range(depth):
                if other != layer:
                    slot = slot + found[offset, other] * (level[offset, other] < level[offset, layer]).astype(jnp.int32)
            slots[offset, layer] = jnp.minimum(slot, pops_ref.shape[0] - 1)
        for layer in range(depth):
            before = before + found[offset, layer]
    start = my_x * (count_y * depth)
    shift0 = lax.rem(owner_ref[start], count_y)
    shift1 = lax.rem(owner_ref[start + 1], count_y)
    low, high = jnp.minimum(shift0, shift1), jnp.maximum(shift0, shift1)
    meta_ref[0] = pair_index(low, high, count_y)
    meta_ref[1] = (shift0 > shift1).astype(jnp.int32)
    meta_ref[2] = odd
    for layer, shift in ((0, shift0), (1, shift1)):
        row = lax.rem(my_y - shift + count_y, count_y)
        source = owner_ref[start + row * depth + layer] // count_y - my_x
        meta_ref[3 + layer] = jnp.where(source == 0, 0, jnp.where(source == 1 - 2 * odd, 1, 2))
    rate_copy.wait()
    solid_copy.wait()
    narrow = lane_of((1, LANES)) < 64
    for tile in range(TILES):
        flags = jnp.where(solid_ref[:, tile * LANES:(tile + 1) * LANES] == 1, 1.0, 0.0)
        lower, upper = flags[0:1, :], flags[1:2, :]
        extra_ref[pl.ds(2 * tile, 1), :] = jnp.where(narrow, lower, roll(upper, 64, 1))
        extra_ref[pl.ds(2 * tile + 1, 1), :] = jnp.where(narrow, roll(lower, 64, 1), upper)
    extra_ref[pl.ds(EDGE, EDGE), :] = jnp.where(lane_of((EDGE, LANES)) < 64, rate_ref[0], rate_ref[1])
    pops_copy.wait()
    for layer in range(depth):
        left, right = slots[-1, layer], slots[1, layer]
        one = jnp.where(odd == 1, left, right)
        two = jnp.where(odd == 1, right, left)
        meta_ref[5 + layer] = slots[0, layer]
        for ref, slot in ((one_ref, one), (two_ref, two)):
            for tile in range(TILES):
                ref[pl.ds(layer * ROWS + tile * POPS, POPS), :] = pops_ref[slot, :, tile * LANES:(tile + 1) * LANES]


def select_kernel(meta_ref, pops_ref, one_ref, two_ref, low_ref, high_ref):
    swapped = meta_ref[1] == 1
    for tile in range(TILES):
        blocks = []
        for layer in range(2):
            source = meta_ref[3 + layer]
            part = pl.ds(layer * ROWS + tile * POPS, POPS)
            keep = pops_ref[meta_ref[5 + layer], :, tile * LANES:(tile + 1) * LANES]
            blocks.append(jnp.where(source == 0, keep, jnp.where(source == 1, one_ref[part, :], two_ref[part, :])))
        low_ref[pl.ds(tile * POPS, POPS), :] = jnp.where(swapped, blocks[1], blocks[0])
        high_ref[pl.ds(tile * POPS, POPS), :] = jnp.where(swapped, blocks[0], blocks[1])


def collide_kernel(meta_ref, extra_ref, low_ref, high_ref, state_ref, one_ref, two_ref):
    swapped = meta_ref[1] == 1
    odd = meta_ref[2] == 1
    wide = lane_of((POPS, LANES)) < 64
    for tile in range(TILES):
        part = pl.ds(tile * POPS, POPS)
        low, high = low_ref[part, :], high_ref[part, :]
        lower = jnp.where(swapped, high, low)
        upper = jnp.where(swapped, low, high)
        state_ref[pl.ds(2 * tile, POPS, stride=EDGE), :] = jnp.where(wide, lower, roll(upper, 64, 1))
        state_ref[pl.ds(2 * tile + 1, POPS, stride=EDGE), :] = jnp.where(wide, roll(lower, 64, 1), upper)
    state_ref[pl.ds(SOLID * EDGE, 2 * EDGE), :] = extra_ref[...]
    rate = extra_ref[pl.ds(EDGE, EDGE), :]
    solid = extra_ref[pl.ds(0, EDGE), :] > 0.5
    pops = [state_ref[pl.ds(q * EDGE, EDGE), :] for q in range(POPS)]
    for q, value in enumerate(collide(pops, rate, solid)):
        state_ref[pl.ds(q * EDGE, EDGE), :] = value
    for count, place, mine, theirs in ((CHANNELS, 0, EDGE - 1, 0), (POPS, CHANNELS, EDGE - 2, 1)):
        right = state_ref[pl.ds(mine, count, stride=EDGE), :]
        left = state_ref[pl.ds(theirs, count, stride=EDGE), :]
        one_ref[pl.ds(place, count), :] = jnp.where(odd, left, right)
        two_ref[pl.ds(place, count), :] = jnp.where(odd, right, left)


def extend(meta_ref, state_ref, one_ref, two_ref, wide_ref):
    odd = meta_ref[2] == 1
    for channel in range(CHANNELS):
        wide_ref[pl.ds(channel * SPAN + 4, EDGE), :] = state_ref[pl.ds(channel * EDGE, EDGE), :]
    for count, place, low, high in ((CHANNELS, 0, 3, 12), (POPS, CHANNELS, 2, 13)):
        one, two = one_ref[pl.ds(place, count), :], two_ref[pl.ds(place, count), :]
        wide_ref[pl.ds(low, count, stride=SPAN), :] = jnp.where(odd, one, two)
        wide_ref[pl.ds(high, count, stride=SPAN), :] = jnp.where(odd, two, one)


def pack_kernel(meta_ref, state_ref, one_ref, two_ref, down_ref, up_ref, wide_ref):
    extend(meta_ref, state_ref, one_ref, two_ref, wide_ref)
    part = lane_of((SPAN, LANES)) // 16
    for ref, first in ((down_ref, 0), (up_ref, 48)):
        for group in range(GROUPS):
            packed = None
            for k in range(4):
                channel = group * 4 + k
                if channel >= CHANNELS:
                    continue
                value = wide_ref[pl.ds(channel * SPAN, SPAN), :]
                for layer in range(2):
                    moved = roll(value, k * 32 + layer * 16 - (layer * 64 + first), 1)
                    packed = moved if packed is None else jnp.where(part == 2 * k + layer, moved, packed)
            ref[pl.ds(group * SPAN, SPAN), :] = packed


def stream(fields, depth_place):
    moved = [[None] * POPS for _ in fields]
    for q in range(POPS):
        step_x, step_y, step_z = VELOCITY[q]
        for layer in range(2):
            value = roll(fields[layer][q], 8 * step_y + step_z, 1)
            if step_z != 0:
                outer = roll(fields[1 - layer][q], 8 * step_y - 7 * step_z, 1)
                value = jnp.where(depth_place == (0 if step_z > 0 else 7), outer, value)
            moved[layer][q] = roll(value, step_x, 0)
    return moved


def finish_kernel(meta_ref, state_ref, one_ref, two_ref, below_ref, above_ref, out_ref, wide_ref, last_ref):
    extend(meta_ref, state_ref, one_ref, two_ref, wide_ref)
    lane = lane_of((SPAN, LANES))
    place = lane % 8
    at_low = (lane >= 16) & (lane < 32)
    at_high = (lane >= 96) & (lane < 112)
    fields = [[None] * CHANNELS for _ in range(2)]
    for channel in range(CHANNELS):
        group, k = divmod(channel, 4)
        value = wide_ref[pl.ds(channel * SPAN, SPAN), :]
        below = below_ref[pl.ds(group * SPAN, SPAN), :]
        above = above_ref[pl.ds(group * SPAN, SPAN), :]
        for layer in range(2):
            at = k * 32 + layer * 16
            field = roll(value, 32 - 64 * layer, 1)
            field = jnp.where(at_low, roll(below, 16 - at, 1), field)
            fields[layer][channel] = jnp.where(at_high, roll(above, 96 - at, 1), field)
    moved = stream([field[:POPS] for field in fields], place)
    relaxed = [collide(moved[layer], fields[layer][RATE], fields[layer][SOLID] > 0.5) for layer in range(2)]
    final = stream(relaxed, place)
    half = lane_of((POPS, LANES)) < 64
    for layer in range(2):
        for q in range(POPS):
            last_ref[layer, pl.ds(q * SPAN, SPAN), :] = final[layer][q]
        for tile in range(TILES):
            even = last_ref[layer, pl.ds(2 * tile + 4, POPS, stride=SPAN), :]
            odd = last_ref[layer, pl.ds(2 * tile + 5, POPS, stride=SPAN), :]
            out_ref[pl.ds(2 * tile + layer, POPS, stride=2 * TILES), :] = jnp.where(half, roll(even, -32, 1), roll(odd, 32, 1))


def shape_of(*dims, dtype=jnp.float32):
    return jax.ShapeDtypeStruct(dims, dtype)


def local(pops_old, old_owner, relax, solid_mask):
    count_x, count_y = lax.axis_size("bx"), lax.axis_size("by")
    depth = relax.shape[0]
    inside = [pair for k in range(0, count_x, 2) for pair in ((k, k + 1), (k + 1, k))]
    across = [
        pair for k in range(1, count_x, 2) for pair in ((k, (k + 1) % count_x), ((k + 1) % count_x, k))
    ]
    up = [(k, (k + 1) % count_y) for k in range(count_y)]
    down = [(k, (k - 1) % count_y) for k in range(count_y)]

    one, two, extra, meta = pl.pallas_call(
        functools.partial(gather_kernel, count_x, count_y, depth),
        out_shape=[shape_of(depth * ROWS, LANES)] * 2
        + [shape_of(2 * EDGE, LANES), shape_of(8, dtype=jnp.int32)],
        in_specs=[HBM] * 4,
        out_specs=[VMEM] * 3 + [SMEM],
        scratch_shapes=[
            pltpu.SMEM(old_owner.shape, jnp.int32),
            pltpu.VMEM(pops_old.shape, jnp.float32),
            pltpu.SMEM(relax.shape, jnp.float32),
            pltpu.VMEM(solid_mask.shape, jnp.int32),
            pltpu.SemaphoreType.DMA((4,)),
        ],
        name="gather_blocks",
    )(old_owner, pops_old, relax, solid_mask)
    two = lax.ppermute(two, "bx", across)
    one = lax.ppermute(one, "bx", inside)
    low, high = pl.pallas_call(
        select_kernel,
        out_shape=[shape_of(ROWS, LANES)] * 2,
        in_specs=[SMEM, VMEM, VMEM, VMEM],
        out_specs=[VMEM, VMEM],
        compiler_params=SMALL,
        name="select_blocks",
    )(meta, pops_old, one, two)

    def shifted(block, shift):
        if shift % count_y == 0:
            return block
        return lax.ppermute(block, "by", [((k + shift) % count_y, k) for k in range(count_y)])

    def branch(first, second):
        def hops(shift):
            return min(shift % count_y, -shift % count_y)

        gap = second - first
        plans = [(hops(first) + hops(second), None)]
        plans.append((hops(gap) + hops(first) + 4.5, (0, gap, first)))
        plans.append((hops(gap) + hops(second) + 4.5, (-gap, 0, second)))
        plan = min(plans, key=lambda entry: entry[0])[1]

        def move(low, high):
            if plan is None or 0 in (first, second):
                return shifted(low, first), shifted(high, second)
            low, high = shifted(low, plan[0]), shifted(high, plan[1])
            both = shifted(jnp.concatenate([low, high]), plan[2])
            return both[:ROWS], both[ROWS:]

        return move

    pairs = [(first, second) for first in range(count_y) for second in range(first + 1, count_y)]
    low, high = lax.switch(meta[0], [branch(*pair) for pair in pairs], low, high)

    state, one, two = pl.pallas_call(
        collide_kernel,
        out_shape=[shape_of(CHANNELS * EDGE, LANES)] + [shape_of(CHANNELS + POPS, LANES)] * 2,
        in_specs=[SMEM, VMEM, VMEM, VMEM],
        out_specs=[VMEM] * 3,
        compiler_params=SMALL,
        name="collide_first",
    )(meta, extra, low, high)
    two = lax.ppermute(two, "bx", across)
    one = lax.ppermute(one, "bx", inside)
    to_below, to_above = pl.pallas_call(
        pack_kernel,
        out_shape=[shape_of(GROUPS * SPAN, LANES)] * 2,
        in_specs=[SMEM, VMEM, VMEM, VMEM],
        out_specs=[VMEM] * 2,
        scratch_shapes=[pltpu.VMEM((CHANNELS * SPAN, LANES), jnp.float32)],
        compiler_params=SMALL,
        name="pack_faces",
    )(meta, state, one, two)
    below = lax.ppermute(to_above, "by", up)
    above = lax.ppermute(to_below, "by", down)
    rows = pl.pallas_call(
        finish_kernel,
        out_shape=shape_of(POPS * TILES * depth, LANES),
        in_specs=[SMEM] + [VMEM] * 5,
        out_specs=VMEM,
        scratch_shapes=[
            pltpu.VMEM((CHANNELS * SPAN, LANES), jnp.float32),
            pltpu.VMEM((2, POPS * SPAN, LANES), jnp.float32),
        ],
        compiler_params=SMALL,
        name="stream_collide_stream",
    )(meta, state, one, two, below, above)
    return (
        rows.reshape(POPS, TILES, depth, LANES).transpose(2, 0, 1, 3).reshape(depth, POPS, TILES * LANES)
    )


def solution(mesh):
    return jax.shard_map(
        local,
        mesh=mesh,
        in_specs=(P(("bx", "by"), None, None), P(), P(("bx", "by")), P(("bx", "by"), None)),
        out_specs=P(("bx", "by"), None, None),
        check_vma=False,
    )
```

```python
import functools

import jax
import jax.numpy as jnp
import numpy as np
from jax import lax
from jax.experimental import pallas as pl
from jax.experimental.pallas import tpu as pltpu
from jax.sharding import PartitionSpec as P

EDGE = 8
POPS = 19
TILES = 4
LANES = 128
ROWS = POPS * TILES
CHANNELS = POPS + 2
SOLID = POPS
RATE = POPS + 1
SPAN = 16
GROUPS = (CHANNELS + 3) // 4

VELOCITY = (
    (0, 0, 0), (1, 0, 0), (-1, 0, 0), (0, 1, 0), (0, -1, 0), (0, 0, 1), (0, 0, -1),
    (1, 1, 0), (-1, -1, 0), (1, -1, 0), (-1, 1, 0), (1, 0, 1), (-1, 0, -1), (1, 0, -1),
    (-1, 0, 1), (0, 1, 1), (0, -1, -1), (0, 1, -1), (0, -1, 1),
)
WEIGHTS = (1.0 / 3.0,) + (1.0 / 18.0,) * 6 + (1.0 / 36.0,) * 12
MAGIC_TRT = 0.1875
RELAY = 5.5

VMEM = pl.BlockSpec(memory_space=pltpu.VMEM)
SMEM = pl.BlockSpec(memory_space=pltpu.SMEM)
HBM = pl.BlockSpec(memory_space=pltpu.HBM)
SMALL = pltpu.CompilerParams(vmem_limit_bytes=4 * 1024 * 1024)


def roll(value, shift, axis):
    size = value.shape[axis]
    shift = shift % size
    return value if shift == 0 else pltpu.roll(value, shift, axis)


def lane_of(shape):
    return lax.broadcasted_iota(jnp.int32, shape, len(shape) - 1)


def pair_index(low, high, count):
    return low * (2 * count - low - 1) // 2 + (high - low - 1)


def collide(pops, rate, solid):
    rho = functools.reduce(jnp.add, pops)
    flux = []
    for axis in range(3):
        plus = functools.reduce(jnp.add, [pops[q] for q in range(POPS) if VELOCITY[q][axis] > 0])
        minus = functools.reduce(jnp.add, [pops[q] for q in range(POPS) if VELOCITY[q][axis] < 0])
        flux.append(plus - minus)
    base = rho - 1.5 * (flux[0] * flux[0] + flux[1] * flux[1] + flux[2] * flux[2])
    rate_odd = 1.0 / (MAGIC_TRT / (1.0 / rate - 0.5) + 0.5)
    relaxed = [None] * POPS
    rest = pops[0] - rate * (pops[0] - WEIGHTS[0] * base)
    relaxed[0] = jnp.where(solid, pops[0], rest)
    for q in range(1, POPS, 2):
        one, two = pops[q], pops[q + 1]
        speed = None
        for axis in range(3):
            if VELOCITY[q][axis] != 0:
                term = flux[axis] if VELOCITY[q][axis] > 0 else -flux[axis]
                speed = term if speed is None else speed + term
        even = rate * (0.5 * (one + two) - WEIGHTS[q] * (base + 4.5 * speed * speed))
        odd = rate_odd * (0.5 * (one - two) - (3.0 * WEIGHTS[q]) * speed)
        relaxed[q] = jnp.where(solid, two, one - even - odd)
        relaxed[q + 1] = jnp.where(solid, one, two - even + odd)
    return relaxed


def gather_kernel(
    count_x, count_y, depth, owner_in, pops_in, rate_in, solid_in,
    one_ref, two_ref, extra_ref, meta_ref,
    owner_ref, pops_ref, rate_ref, solid_ref, sems,
):
    owner_copy = pltpu.make_async_copy(owner_in, owner_ref, sems.at[0])
    pops_copy = pltpu.make_async_copy(pops_in, pops_ref, sems.at[1])
    rate_copy = pltpu.make_async_copy(rate_in, rate_ref, sems.at[2])
    solid_copy = pltpu.make_async_copy(solid_in, solid_ref, sems.at[3])
    owner_copy.start()
    pops_copy.start()
    rate_copy.start()
    solid_copy.start()
    owner_copy.wait()
    my_x, my_y = lax.axis_index("bx"), lax.axis_index("by")
    myself = my_x * count_y + my_y
    odd = lax.rem(my_x, 2)
    found, level = {}, {}
    for offset in (-1, 0, 1):
        place = my_x + offset
        inside = (place >= 0) & (place < count_x)
        start = jnp.clip(place, 0, count_x - 1) * (count_y * depth)
        for layer in range(depth):
            shift = lax.rem(owner_ref[start + layer], count_y)
            row = lax.rem(my_y - shift + count_y, count_y)
            hit = (owner_ref[start + row * depth + layer] == myself) & inside
            found[offset, layer] = hit.astype(jnp.int32)
            level[offset, layer] = row * depth + layer
    slots = {}
    before = jnp.int32(0)
    for offset in (-1, 0, 1):
        for layer in range(depth):
            slot = before
            for other in range(depth):
                if other != layer:
                    slot = slot + found[offset, other] * (level[offset, other] < level[offset, layer]).astype(jnp.int32)
            slots[offset, layer] = jnp.minimum(slot, pops_ref.shape[0] - 1)
        for layer in range(depth):
            before = before + found[offset, layer]
    start = my_x * (count_y * depth)
    shift0 = lax.rem(owner_ref[start], count_y)
    shift1 = lax.rem(owner_ref[start + 1], count_y)
    low, high = jnp.minimum(shift0, shift1), jnp.maximum(shift0, shift1)
    meta_ref[0] = pair_index(low, high, count_y)
    hops0, hops1 = jnp.minimum(shift0, count_y - shift0), jnp.minimum(shift1, count_y - shift1)
    meta_ref[1] = ((hops1 > hops0) | ((hops1 == hops0) & (shift1 < shift0))).astype(jnp.int32)
    meta_ref[2] = odd
    for layer, shift in ((0, shift0), (1, shift1)):
        row = lax.rem(my_y - shift + count_y, count_y)
        source = owner_ref[start + row * depth + layer] // count_y - my_x
        meta_ref[3 + layer] = jnp.where(source == 0, 0, jnp.where(source == 1 - 2 * odd, 1, 2))
    rate_copy.wait()
    solid_copy.wait()
    narrow = lane_of((1, LANES)) < 64
    for tile in range(TILES):
        flags = jnp.where(solid_ref[:, tile * LANES:(tile + 1) * LANES] == 1, 1.0, 0.0)
        lower, upper = flags[0:1, :], flags[1:2, :]
        extra_ref[pl.ds(2 * tile, 1), :] = jnp.where(narrow, lower, roll(upper, 64, 1))
        extra_ref[pl.ds(2 * tile + 1, 1), :] = jnp.where(narrow, roll(lower, 64, 1), upper)
    extra_ref[pl.ds(EDGE, EDGE), :] = jnp.where(lane_of((EDGE, LANES)) < 64, rate_ref[0], rate_ref[1])
    pops_copy.wait()
    for layer in range(depth):
        left, right = slots[-1, layer], slots[1, layer]
        one = jnp.where(odd == 1, left, right)
        two = jnp.where(odd == 1, right, left)
        meta_ref[5 + layer] = slots[0, layer]
        for ref, slot in ((one_ref, one), (two_ref, two)):
            for tile in range(TILES):
                ref[pl.ds(layer * ROWS + tile * POPS, POPS), :] = pops_ref[slot, :, tile * LANES:(tile + 1) * LANES]


def select_kernel(meta_ref, pops_ref, two_ref, one_ref, near_ref, far_ref):
    swapped = meta_ref[1] == 1
    for tile in range(TILES):
        blocks = []
        for layer in range(2):
            source = meta_ref[3 + layer]
            part = pl.ds(layer * ROWS + tile * POPS, POPS)
            keep = pops_ref[meta_ref[5 + layer], :, tile * LANES:(tile + 1) * LANES]
            blocks.append(jnp.where(source == 0, keep, jnp.where(source == 1, one_ref[part, :], two_ref[part, :])))
        far_ref[pl.ds(tile * POPS, POPS), :] = jnp.where(swapped, blocks[1], blocks[0])
        near_ref[pl.ds(tile * POPS, POPS), :] = jnp.where(swapped, blocks[0], blocks[1])


def collide_kernel(meta_ref, extra_ref, near_ref, far_ref, state_ref, one_ref, two_ref):
    swapped = meta_ref[1] == 1
    odd = meta_ref[2] == 1
    wide = lane_of((POPS, LANES)) < 64
    for tile in range(TILES):
        part = pl.ds(tile * POPS, POPS)
        far, near = far_ref[part, :], near_ref[part, :]
        lower = jnp.where(swapped, near, far)
        upper = jnp.where(swapped, far, near)
        state_ref[pl.ds(2 * tile, POPS, stride=EDGE), :] = jnp.where(wide, lower, roll(upper, 64, 1))
        state_ref[pl.ds(2 * tile + 1, POPS, stride=EDGE), :] = jnp.where(wide, roll(lower, 64, 1), upper)
    state_ref[pl.ds(SOLID * EDGE, 2 * EDGE), :] = extra_ref[...]
    rate = extra_ref[pl.ds(EDGE, EDGE), :]
    solid = extra_ref[pl.ds(0, EDGE), :] > 0.5
    pops = [state_ref[pl.ds(q * EDGE, EDGE), :] for q in range(POPS)]
    for q, value in enumerate(collide(pops, rate, solid)):
        state_ref[pl.ds(q * EDGE, EDGE), :] = value
    for count, place, mine, theirs in ((CHANNELS, 0, EDGE - 1, 0), (POPS, CHANNELS, EDGE - 2, 1)):
        right = state_ref[pl.ds(mine, count, stride=EDGE), :]
        left = state_ref[pl.ds(theirs, count, stride=EDGE), :]
        one_ref[pl.ds(place, count), :] = jnp.where(odd, left, right)
        two_ref[pl.ds(place, count), :] = jnp.where(odd, right, left)


def extend(meta_ref, state_ref, one_ref, two_ref, wide_ref):
    odd = meta_ref[2] == 1
    for channel in range(CHANNELS):
        wide_ref[pl.ds(channel * SPAN + 4, EDGE), :] = state_ref[pl.ds(channel * EDGE, EDGE), :]
    for count, place, low, high in ((CHANNELS, 0, 3, 12), (POPS, CHANNELS, 2, 13)):
        one, two = one_ref[pl.ds(place, count), :], two_ref[pl.ds(place, count), :]
        wide_ref[pl.ds(low, count, stride=SPAN), :] = jnp.where(odd, one, two)
        wide_ref[pl.ds(high, count, stride=SPAN), :] = jnp.where(odd, two, one)


def pack_kernel(meta_ref, state_ref, two_ref, one_ref, down_ref, up_ref, wide_ref):
    extend(meta_ref, state_ref, one_ref, two_ref, wide_ref)
    part = lane_of((SPAN, LANES)) // 16
    for ref, first in ((down_ref, 0), (up_ref, 48)):
        for group in range(GROUPS):
            packed = None
            for k in range(4):
                channel = group * 4 + k
                if channel >= CHANNELS:
                    continue
                value = wide_ref[pl.ds(channel * SPAN, SPAN), :]
                for layer in range(2):
                    moved = roll(value, k * 32 + layer * 16 - (layer * 64 + first), 1)
                    packed = moved if packed is None else jnp.where(part == 2 * k + layer, moved, packed)
            ref[pl.ds(group * SPAN, SPAN), :] = packed


def stream(fields, depth_place):
    moved = [[None] * POPS for _ in fields]
    for q in range(POPS):
        step_x, step_y, step_z = VELOCITY[q]
        for layer in range(2):
            value = roll(fields[layer][q], 8 * step_y + step_z, 1)
            if step_z != 0:
                outer = roll(fields[1 - layer][q], 8 * step_y - 7 * step_z, 1)
                value = jnp.where(depth_place == (0 if step_z > 0 else 7), outer, value)
            moved[layer][q] = roll(value, step_x, 0)
    return moved


def finish_kernel(meta_ref, state_ref, two_ref, one_ref, befar_ref, above_ref, out_ref, wide_ref, last_ref):
    extend(meta_ref, state_ref, one_ref, two_ref, wide_ref)
    lane = lane_of((SPAN, LANES))
    place = lane % 8
    at_low = (lane >= 16) & (lane < 32)
    at_high = (lane >= 96) & (lane < 112)
    fields = [[None] * CHANNELS for _ in range(2)]
    for channel in range(CHANNELS):
        group, k = divmod(channel, 4)
        value = wide_ref[pl.ds(channel * SPAN, SPAN), :]
        below = befar_ref[pl.ds(group * SPAN, SPAN), :]
        above = above_ref[pl.ds(group * SPAN, SPAN), :]
        for layer in range(2):
            at = k * 32 + layer * 16
            field = roll(value, 32 - 64 * layer, 1)
            field = jnp.where(at_low, roll(below, 16 - at, 1), field)
            fields[layer][channel] = jnp.where(at_high, roll(above, 96 - at, 1), field)
    moved = stream([field[:POPS] for field in fields], place)
    relaxed = [collide(moved[layer], fields[layer][RATE], fields[layer][SOLID] > 0.5) for layer in range(2)]
    final = stream(relaxed, place)
    half = lane_of((POPS, LANES)) < 64
    for layer in range(2):
        for q in range(POPS):
            last_ref[layer, pl.ds(q * SPAN, SPAN), :] = final[layer][q]
        for tile in range(TILES):
            even = last_ref[layer, pl.ds(2 * tile + 4, POPS, stride=SPAN), :]
            odd = last_ref[layer, pl.ds(2 * tile + 5, POPS, stride=SPAN), :]
            out_ref[pl.ds(2 * tile + layer, POPS, stride=2 * TILES), :] = jnp.where(half, roll(even, -32, 1), roll(odd, 32, 1))


def shape_of(*dims, dtype=jnp.float32):
    return jax.ShapeDtypeStruct(dims, dtype)


def local(pops_old, old_owner, relax, solid_mask):
    count_x, count_y = lax.axis_size("bx"), lax.axis_size("by")
    depth = relax.shape[0]
    inside = [pair for k in range(0, count_x, 2) for pair in ((k, k + 1), (k + 1, k))]
    across = [
        pair for k in range(1, count_x, 2) for pair in ((k, (k + 1) % count_x), ((k + 1) % count_x, k))
    ]
    up = [(k, (k + 1) % count_y) for k in range(count_y)]
    down = [(k, (k - 1) % count_y) for k in range(count_y)]

    one, two, extra, meta = pl.pallas_call(
        functools.partial(gather_kernel, count_x, count_y, depth),
        out_shape=[shape_of(depth * ROWS, LANES)] * 2
        + [shape_of(2 * EDGE, LANES), shape_of(8, dtype=jnp.int32)],
        in_specs=[HBM] * 4,
        out_specs=[VMEM] * 3 + [SMEM],
        scratch_shapes=[
            pltpu.SMEM(old_owner.shape, jnp.int32),
            pltpu.VMEM(pops_old.shape, jnp.float32),
            pltpu.SMEM(relax.shape, jnp.float32),
            pltpu.VMEM(solid_mask.shape, jnp.int32),
            pltpu.SemaphoreType.DMA((4,)),
        ],
        name="gather_blocks",
    )(old_owner, pops_old, relax, solid_mask)
    two = lax.ppermute(two, "bx", across)
    one = lax.ppermute(one, "bx", inside)
    near, far = pl.pallas_call(
        select_kernel,
        out_shape=[shape_of(ROWS, LANES)] * 2,
        in_specs=[SMEM, VMEM, VMEM, VMEM],
        out_specs=[VMEM, VMEM],
        compiler_params=SMALL,
        name="select_blocks",
    )(meta, pops_old, two, one)

    def hops(shift):
        return min(shift % count_y, -shift % count_y)

    def shifted(block, shift):
        if shift % count_y == 0:
            return block
        return lax.ppermute(block, "by", [((k + shift) % count_y, k) for k in range(count_y)])

    def branch(low, high):
        first, second = (high, low) if hops(high) > hops(low) else (low, high)
        plans = [
            (hops(first) + hops(second), None),
            (hops(second - first) + hops(first) + RELAY, (0, second - first, first)),
            (hops(first - second) + hops(second) + RELAY, (first - second, 0, second)),
        ]
        plan = min(plans, key=lambda entry: entry[0])[1]

        def move(near, far):
            if plan is None:
                return shifted(near, second), shifted(far, first)
            both = shifted(jnp.concatenate([shifted(near, plan[1]), shifted(far, plan[0])]), plan[2])
            return both[:ROWS], both[ROWS:]

        return move

    pairs = [(low, high) for low in range(count_y) for high in range(low + 1, count_y)]
    near, far = lax.switch(meta[0], [branch(*pair) for pair in pairs], near, far)

    state, one, two = pl.pallas_call(
        collide_kernel,
        out_shape=[shape_of(CHANNELS * EDGE, LANES)] + [shape_of(CHANNELS + POPS, LANES)] * 2,
        in_specs=[SMEM, VMEM, VMEM, VMEM],
        out_specs=[VMEM] * 3,
        compiler_params=SMALL,
        name="collide_first",
    )(meta, extra, near, far)
    two = lax.ppermute(two, "bx", across)
    one = lax.ppermute(one, "bx", inside)
    to_below, to_above = pl.pallas_call(
        pack_kernel,
        out_shape=[shape_of(GROUPS * SPAN, LANES)] * 2,
        in_specs=[SMEM, VMEM, VMEM, VMEM],
        out_specs=[VMEM] * 2,
        scratch_shapes=[pltpu.VMEM((CHANNELS * SPAN, LANES), jnp.float32)],
        compiler_params=SMALL,
        name="pack_faces",
    )(meta, state, two, one)
    below = lax.ppermute(to_above, "by", up)
    above = lax.ppermute(to_below, "by", down)
    rows = pl.pallas_call(
        finish_kernel,
        out_shape=shape_of(POPS * TILES * depth, LANES),
        in_specs=[SMEM] + [VMEM] * 5,
        out_specs=VMEM,
        scratch_shapes=[
            pltpu.VMEM((CHANNELS * SPAN, LANES), jnp.float32),
            pltpu.VMEM((2, POPS * SPAN, LANES), jnp.float32),
        ],
        compiler_params=SMALL,
        name="stream_collide_stream",
    )(meta, state, two, one, below, above)
    return (
        rows.reshape(POPS, TILES, depth, LANES).transpose(2, 0, 1, 3).reshape(depth, POPS, TILES * LANES)
    )


def solution(mesh):
    return jax.shard_map(
        local,
        mesh=mesh,
        in_specs=(P(("bx", "by"), None, None), P(), P(("bx", "by")), P(("bx", "by"), None)),
        out_specs=P(("bx", "by"), None, None),
        check_vma=False,
    )
```

```python
import functools

import jax
import jax.numpy as jnp
import numpy as np
from jax import lax
from jax.experimental import pallas as pl
from jax.experimental.pallas import tpu as pltpu
from jax.sharding import PartitionSpec as P

EDGE = 8
POPS = 19
TILES = 4
LANES = 128
ROWS = POPS * TILES
CHANNELS = POPS + 2
SOLID = POPS
RATE = POPS + 1
SPAN = 16
INWARD = 5
SLOTS = CHANNELS + INWARD
GROUPS = (SLOTS + 7) // 8

VELOCITY = (
    (0, 0, 0), (1, 0, 0), (-1, 0, 0), (0, 1, 0), (0, -1, 0), (0, 0, 1), (0, 0, -1),
    (1, 1, 0), (-1, -1, 0), (1, -1, 0), (-1, 1, 0), (1, 0, 1), (-1, 0, -1), (1, 0, -1),
    (-1, 0, 1), (0, 1, 1), (0, -1, -1), (0, 1, -1), (0, -1, 1),
)
WEIGHTS = (1.0 / 3.0,) + (1.0 / 18.0,) * 6 + (1.0 / 36.0,) * 12
MAGIC_TRT = 0.1875
RELAY = 5.5

VMEM = pl.BlockSpec(memory_space=pltpu.VMEM)
SMEM = pl.BlockSpec(memory_space=pltpu.SMEM)
HBM = pl.BlockSpec(memory_space=pltpu.HBM)
SMALL = pltpu.CompilerParams(vmem_limit_bytes=4 * 1024 * 1024)


def roll(value, shift, axis):
    size = value.shape[axis]
    shift = shift % size
    return value if shift == 0 else pltpu.roll(value, shift, axis)


def parity():
    return lax.rem(lax.axis_index("bx"), 2) == 1


def moving(axis, sign):
    return [q for q in range(POPS) if VELOCITY[q][axis] == sign]


def lane_of(shape):
    return lax.broadcasted_iota(jnp.int32, shape, len(shape) - 1)


def pair_index(low, high, count):
    return low * (2 * count - low - 1) // 2 + (high - low - 1)


def collide(pops, rate, solid):
    rho = functools.reduce(jnp.add, pops)
    flux = []
    for axis in range(3):
        plus = functools.reduce(jnp.add, [pops[q] for q in range(POPS) if VELOCITY[q][axis] > 0])
        minus = functools.reduce(jnp.add, [pops[q] for q in range(POPS) if VELOCITY[q][axis] < 0])
        flux.append(plus - minus)
    base = rho - 1.5 * (flux[0] * flux[0] + flux[1] * flux[1] + flux[2] * flux[2])
    rate_odd = 1.0 / (MAGIC_TRT / (1.0 / rate - 0.5) + 0.5)
    relaxed = [None] * POPS
    rest = pops[0] - rate * (pops[0] - WEIGHTS[0] * base)
    relaxed[0] = jnp.where(solid, pops[0], rest)
    for q in range(1, POPS, 2):
        one, two = pops[q], pops[q + 1]
        speed = None
        for axis in range(3):
            if VELOCITY[q][axis] != 0:
                term = flux[axis] if VELOCITY[q][axis] > 0 else -flux[axis]
                speed = term if speed is None else speed + term
        even = rate * (0.5 * (one + two) - WEIGHTS[q] * (base + 4.5 * speed * speed))
        odd = rate_odd * (0.5 * (one - two) - (3.0 * WEIGHTS[q]) * speed)
        relaxed[q] = jnp.where(solid, two, one - even - odd)
        relaxed[q + 1] = jnp.where(solid, one, two - even + odd)
    return relaxed


def gather_kernel(
    count_x, count_y, depth, owner_in, pops_in, rate_in, solid_in,
    one_ref, two_ref, extra_ref, index_ref,
    owner_ref, pops_ref, rate_ref, solid_ref, sems,
):
    owner_copy = pltpu.make_async_copy(owner_in, owner_ref, sems.at[0])
    pops_copy = pltpu.make_async_copy(pops_in, pops_ref, sems.at[1])
    rate_copy = pltpu.make_async_copy(rate_in, rate_ref, sems.at[2])
    solid_copy = pltpu.make_async_copy(solid_in, solid_ref, sems.at[3])
    owner_copy.start()
    pops_copy.start()
    rate_copy.start()
    solid_copy.start()
    owner_copy.wait()
    my_x, my_y = lax.axis_index("bx"), lax.axis_index("by")
    myself = my_x * count_y + my_y
    odd = lax.rem(my_x, 2)
    found, level = {}, {}
    for offset in (-1, 0, 1):
        place = my_x + offset
        inside = (place >= 0) & (place < count_x)
        start = jnp.clip(place, 0, count_x - 1) * (count_y * depth)
        for layer in range(depth):
            shift = lax.rem(owner_ref[start + layer], count_y)
            row = lax.rem(my_y - shift + count_y, count_y)
            hit = (owner_ref[start + row * depth + layer] == myself) & inside
            found[offset, layer] = hit.astype(jnp.int32)
            level[offset, layer] = row * depth + layer
    slots = {}
    before = jnp.int32(0)
    for offset in (-1, 0, 1):
        for layer in range(depth):
            slot = before
            for other in range(depth):
                if other != layer:
                    slot = slot + found[offset, other] * (level[offset, other] < level[offset, layer]).astype(jnp.int32)
            slots[offset, layer] = jnp.minimum(slot, pops_ref.shape[0] - 1)
        for layer in range(depth):
            before = before + found[offset, layer]
    start = my_x * (count_y * depth)
    shift0 = lax.rem(owner_ref[start], count_y)
    shift1 = lax.rem(owner_ref[start + 1], count_y)
    low, high = jnp.minimum(shift0, shift1), jnp.maximum(shift0, shift1)
    index_ref[0] = pair_index(low, high, count_y)
    hops0, hops1 = jnp.minimum(shift0, count_y - shift0), jnp.minimum(shift1, count_y - shift1)
    flags = [(hops1 > hops0) | ((hops1 == hops0) & (shift1 < shift0))]
    for layer, shift in ((0, shift0), (1, shift1)):
        row = lax.rem(my_y - shift + count_y, count_y)
        source = owner_ref[start + row * depth + layer] // count_y - my_x
        flags.append(jnp.where(source == 0, 0, jnp.where(source == 1 - 2 * odd, 1, 2)))
    flags += [slots[0, layer] for layer in range(depth)]
    for k, flag in enumerate(flags):
        extra_ref[pl.ds(2 * EDGE + k, 1), :] = jnp.full((1, LANES), flag.astype(jnp.float32))
    rate_copy.wait()
    solid_copy.wait()
    narrow = lane_of((1, LANES)) < 64
    for tile in range(TILES):
        flags = jnp.where(solid_ref[:, tile * LANES:(tile + 1) * LANES] == 1, 1.0, 0.0)
        lower, upper = flags[0:1, :], flags[1:2, :]
        extra_ref[pl.ds(2 * tile, 1), :] = jnp.where(narrow, lower, roll(upper, 64, 1))
        extra_ref[pl.ds(2 * tile + 1, 1), :] = jnp.where(narrow, roll(lower, 64, 1), upper)
    extra_ref[pl.ds(EDGE, EDGE), :] = jnp.where(lane_of((EDGE, LANES)) < 64, rate_ref[0], rate_ref[1])
    pops_copy.wait()
    for layer in range(depth):
        left, right = slots[-1, layer], slots[1, layer]
        one = jnp.where(odd == 1, left, right)
        two = jnp.where(odd == 1, right, left)
        for ref, slot in ((one_ref, one), (two_ref, two)):
            for tile in range(TILES):
                ref[pl.ds(layer * ROWS + tile * POPS, POPS), :] = pops_ref[slot, :, tile * LANES:(tile + 1) * LANES]


def select_kernel(extra_ref, pops_ref, two_ref, one_ref, near_ref, far_ref):
    flags = [extra_ref[pl.ds(2 * EDGE + k, 1), :] for k in range(5)]
    swapped = flags[0] > 0.5
    for tile in range(TILES):
        blocks = []
        for layer in range(2):
            source, slot = flags[1 + layer], flags[3 + layer]
            part = pl.ds(layer * ROWS + tile * POPS, POPS)
            block = jnp.where(source > 1.5, two_ref[part, :], one_ref[part, :])
            for k in range(pops_ref.shape[0]):
                keep = pops_ref[k, :, tile * LANES:(tile + 1) * LANES]
                block = jnp.where((source < 0.5) & (jnp.abs(slot - k) < 0.5), keep, block)
            blocks.append(block)
        far_ref[pl.ds(tile * POPS, POPS), :] = jnp.where(swapped, blocks[1], blocks[0])
        near_ref[pl.ds(tile * POPS, POPS), :] = jnp.where(swapped, blocks[0], blocks[1])


def collide_kernel(extra_ref, near_ref, far_ref, state_ref, down_ref, up_ref):
    swapped = extra_ref[pl.ds(2 * EDGE, 1), :] > 0.5
    wide = lane_of((POPS, LANES)) < 64
    for tile in range(TILES):
        part = pl.ds(tile * POPS, POPS)
        far, near = far_ref[part, :], near_ref[part, :]
        lower = jnp.where(swapped, near, far)
        upper = jnp.where(swapped, far, near)
        state_ref[pl.ds(2 * tile, POPS, stride=EDGE), :] = jnp.where(wide, lower, roll(upper, 64, 1))
        state_ref[pl.ds(2 * tile + 1, POPS, stride=EDGE), :] = jnp.where(wide, roll(lower, 64, 1), upper)
    flags, rate = extra_ref[pl.ds(0, EDGE), :], extra_ref[pl.ds(EDGE, EDGE), :]
    relaxed = collide([state_ref[pl.ds(q * EDGE, EDGE), :] for q in range(POPS)], rate, flags > 0.5)
    values = relaxed + [flags, rate]
    for channel, value in enumerate(values):
        state_ref[pl.ds(channel * EDGE, EDGE), :] = value
    part = lane_of((EDGE, LANES)) // 8
    for ref, beside, second, sign in ((down_ref, 0, 1, -1), (up_ref, EDGE - 1, EDGE - 2, 1)):
        slots = [(channel, beside) for channel in range(CHANNELS)] + [(q, second) for q in moving(1, sign)]
        for group in range(GROUPS):
            packed = None
            for k, (channel, row) in enumerate(slots[8 * group:8 * group + 8]):
                for layer in range(2):
                    moved = roll(values[channel], (2 * k + layer) * 8 - (layer * 64 + row * 8), 1)
                    packed = moved if packed is None else jnp.where(part == 2 * k + layer, moved, packed)
            ref[pl.ds(group * EDGE, EDGE), :] = packed


def widen_kernel(state_ref, below_ref, above_ref, wide_ref, one_ref, two_ref):
    odd = parity()
    part = lane_of((EDGE, LANES)) // 8
    extras = ((below_ref, 3, 2, moving(1, 1)), (above_ref, 12, 13, moving(1, -1)))
    for channel in range(CHANNELS):
        value = state_ref[pl.ds(channel * EDGE, EDGE), :]
        for layer in range(2):
            field = roll(value, 32 - 64 * layer, 1)
            for ref, beside, second, inward in extras:
                slots = [(channel, beside)]
                if channel in inward:
                    slots.append((CHANNELS + inward.index(channel), second))
                for slot, place in slots:
                    group, k = divmod(slot, 8)
                    halo = ref[pl.ds(group * EDGE, EDGE), :]
                    field = jnp.where(part == place, roll(halo, place * 8 - (2 * k + layer) * 8, 1), field)
            wide_ref[pl.ds((layer * CHANNELS + channel) * SPAN + 4, EDGE), :] = field
    for layer in range(2):
        base = layer * CHANNELS * SPAN + 4
        left = wide_ref[pl.ds(base, CHANNELS, stride=SPAN), :]
        right = wide_ref[pl.ds(base + EDGE - 1, CHANNELS, stride=SPAN), :]
        one_ref[pl.ds(layer * SLOTS, CHANNELS), :] = jnp.where(odd, left, right)
        two_ref[pl.ds(layer * SLOTS, CHANNELS), :] = jnp.where(odd, right, left)
        for k, (to_left, to_right) in enumerate(zip(moving(0, -1), moving(0, 1))):
            left = wide_ref[pl.ds(base + to_left * SPAN + 1, 1), :]
            right = wide_ref[pl.ds(base + to_right * SPAN + EDGE - 2, 1), :]
            one_ref[pl.ds(layer * SLOTS + CHANNELS + k, 1), :] = jnp.where(odd, left, right)
            two_ref[pl.ds(layer * SLOTS + CHANNELS + k, 1), :] = jnp.where(odd, right, left)


def stream(fields, depth_place):
    moved = [[None] * POPS for _ in fields]
    for q in range(POPS):
        step_x, step_y, step_z = VELOCITY[q]
        for layer in range(2):
            value = roll(fields[layer][q], 8 * step_y + step_z, 1)
            if step_z != 0:
                outer = roll(fields[1 - layer][q], 8 * step_y - 7 * step_z, 1)
                value = jnp.where(depth_place == (0 if step_z > 0 else 7), outer, value)
            moved[layer][q] = roll(value, step_x, 0)
    return moved


def finish_kernel(wide_ref, two_ref, one_ref, out_ref, halo_ref, last_ref):
    odd = parity()
    place = lane_of((SPAN, LANES)) % 8
    row = lax.broadcasted_iota(jnp.int32, (SPAN, LANES), 0)
    own = (row >= 4) & (row < 4 + EDGE)
    for layer in range(2):
        base = layer * CHANNELS * SPAN
        one, two = one_ref[pl.ds(layer * SLOTS, CHANNELS), :], two_ref[pl.ds(layer * SLOTS, CHANNELS), :]
        halo_ref[pl.ds(base + 3, CHANNELS, stride=SPAN), :] = jnp.where(odd, one, two)
        halo_ref[pl.ds(base + 4 + EDGE, CHANNELS, stride=SPAN), :] = jnp.where(odd, two, one)
        for k, (to_left, to_right) in enumerate(zip(moving(0, -1), moving(0, 1))):
            second = pl.ds(layer * SLOTS + CHANNELS + k, 1)
            one, two = one_ref[second, :], two_ref[second, :]
            halo_ref[pl.ds(base + to_right * SPAN + 2, 1), :] = jnp.where(odd, one, two)
            halo_ref[pl.ds(base + to_left * SPAN + 5 + EDGE, 1), :] = jnp.where(odd, two, one)
    fields = [[None] * CHANNELS for _ in range(2)]
    for layer in range(2):
        for channel in range(CHANNELS):
            part = pl.ds((layer * CHANNELS + channel) * SPAN, SPAN)
            fields[layer][channel] = jnp.where(own, wide_ref[part, :], halo_ref[part, :])
    moved = stream([field[:POPS] for field in fields], place)
    relaxed = [collide(moved[layer], fields[layer][RATE], fields[layer][SOLID] > 0.5) for layer in range(2)]
    final = stream(relaxed, place)
    half = lane_of((POPS, LANES)) < 64
    for layer in range(2):
        for q in range(POPS):
            last_ref[layer, pl.ds(q * SPAN, SPAN), :] = final[layer][q]
        for tile in range(TILES):
            even = last_ref[layer, pl.ds(2 * tile + 4, POPS, stride=SPAN), :]
            odd = last_ref[layer, pl.ds(2 * tile + 5, POPS, stride=SPAN), :]
            out_ref[pl.ds(2 * tile + layer, POPS, stride=2 * TILES), :] = jnp.where(half, roll(even, -32, 1), roll(odd, 32, 1))


def shape_of(*dims, dtype=jnp.float32):
    return jax.ShapeDtypeStruct(dims, dtype)


def local(pops_old, old_owner, relax, solid_mask):
    count_x, count_y = lax.axis_size("bx"), lax.axis_size("by")
    depth = relax.shape[0]
    inside = [pair for k in range(0, count_x, 2) for pair in ((k, k + 1), (k + 1, k))]
    across = [
        pair for k in range(1, count_x, 2) for pair in ((k, (k + 1) % count_x), ((k + 1) % count_x, k))
    ]
    up = [(k, (k + 1) % count_y) for k in range(count_y)]
    down = [(k, (k - 1) % count_y) for k in range(count_y)]

    one, two, extra, index = pl.pallas_call(
        functools.partial(gather_kernel, count_x, count_y, depth),
        out_shape=[shape_of(depth * ROWS, LANES)] * 2
        + [shape_of(3 * EDGE, LANES), shape_of(1, dtype=jnp.int32)],
        in_specs=[HBM] * 4,
        out_specs=[VMEM] * 3 + [SMEM],
        scratch_shapes=[
            pltpu.SMEM(old_owner.shape, jnp.int32),
            pltpu.VMEM(pops_old.shape, jnp.float32),
            pltpu.SMEM(relax.shape, jnp.float32),
            pltpu.VMEM(solid_mask.shape, jnp.int32),
            pltpu.SemaphoreType.DMA((4,)),
        ],
        name="gather_blocks",
    )(old_owner, pops_old, relax, solid_mask)
    two = lax.ppermute(two, "bx", across)
    one = lax.ppermute(one, "bx", inside)
    near, far = pl.pallas_call(
        select_kernel,
        out_shape=[shape_of(ROWS, LANES)] * 2,
        in_specs=[VMEM] * 4,
        out_specs=[VMEM] * 2,
        compiler_params=SMALL,
        name="select_blocks",
    )(extra, pops_old, two, one)

    def hops(shift):
        return min(shift % count_y, -shift % count_y)

    def shifted(block, shift):
        if shift % count_y == 0:
            return block
        return lax.ppermute(block, "by", [((k + shift) % count_y, k) for k in range(count_y)])

    def branch(low, high):
        first, second = (high, low) if hops(high) > hops(low) else (low, high)
        plans = [
            (hops(first) + hops(second), None),
            (hops(second - first) + hops(first) + RELAY, (0, second - first, first)),
            (hops(first - second) + hops(second) + RELAY, (first - second, 0, second)),
        ]
        plan = min(plans, key=lambda entry: entry[0])[1]

        def move(near, far):
            if plan is None:
                return shifted(near, second), shifted(far, first)
            both = shifted(jnp.concatenate([shifted(near, plan[1]), shifted(far, plan[0])]), plan[2])
            return both[:ROWS], both[ROWS:]

        return move

    pairs = [(low, high) for low in range(count_y) for high in range(low + 1, count_y)]
    near, far = lax.switch(index[0], [branch(*pair) for pair in pairs], near, far)

    state, to_below, to_above = pl.pallas_call(
        collide_kernel,
        out_shape=[shape_of(CHANNELS * EDGE, LANES)] + [shape_of(GROUPS * EDGE, LANES)] * 2,
        in_specs=[VMEM] * 3,
        out_specs=[VMEM] * 3,
        compiler_params=SMALL,
        name="collide_first",
    )(extra, near, far)
    below = lax.ppermute(to_above, "by", up)
    above = lax.ppermute(to_below, "by", down)
    wide, one, two = pl.pallas_call(
        widen_kernel,
        out_shape=[shape_of(2 * CHANNELS * SPAN, LANES)] + [shape_of(2 * SLOTS, LANES)] * 2,
        in_specs=[VMEM] * 3,
        out_specs=[VMEM] * 3,
        compiler_params=SMALL,
        name="widen_pack",
    )(state, below, above)
    two = lax.ppermute(two, "bx", across)
    one = lax.ppermute(one, "bx", inside)
    rows = pl.pallas_call(
        finish_kernel,
        out_shape=shape_of(POPS * TILES * depth, LANES),
        in_specs=[VMEM] * 3,
        out_specs=VMEM,
        scratch_shapes=[
            pltpu.VMEM((2 * CHANNELS * SPAN, LANES), jnp.float32),
            pltpu.VMEM((2, POPS * SPAN, LANES), jnp.float32),
        ],
        compiler_params=SMALL,
        name="stream_collide_stream",
    )(wide, two, one)
    return (
        rows.reshape(POPS, TILES, depth, LANES).transpose(2, 0, 1, 3).reshape(depth, POPS, TILES * LANES)
    )


def solution(mesh):
    return jax.shard_map(
        local,
        mesh=mesh,
        in_specs=(P(("bx", "by"), None, None), P(), P(("bx", "by")), P(("bx", "by"), None)),
        out_specs=P(("bx", "by"), None, None),
        check_vma=False,
    )
```

```python
import functools

import jax
import jax.numpy as jnp
import numpy as np
from jax import lax
from jax.experimental import pallas as pl
from jax.experimental.pallas import tpu as pltpu
from jax.sharding import PartitionSpec as P

EDGE = 8
POPS = 19
TILES = 4
LANES = 128
ROWS = POPS * TILES
CHANNELS = POPS + 2
SOLID = POPS
RATE = POPS + 1
SPAN = 16
INWARD = 5
SLOTS = CHANNELS + INWARD
GROUPS = (SLOTS + 7) // 8

VELOCITY = (
    (0, 0, 0), (1, 0, 0), (-1, 0, 0), (0, 1, 0), (0, -1, 0), (0, 0, 1), (0, 0, -1),
    (1, 1, 0), (-1, -1, 0), (1, -1, 0), (-1, 1, 0), (1, 0, 1), (-1, 0, -1), (1, 0, -1),
    (-1, 0, 1), (0, 1, 1), (0, -1, -1), (0, 1, -1), (0, -1, 1),
)
WEIGHTS = (1.0 / 3.0,) + (1.0 / 18.0,) * 6 + (1.0 / 36.0,) * 12
MAGIC_TRT = 0.1875

VMEM = pl.BlockSpec(memory_space=pltpu.VMEM)
SMEM = pl.BlockSpec(memory_space=pltpu.SMEM)
HBM = pl.BlockSpec(memory_space=pltpu.HBM)
SMALL = pltpu.CompilerParams(vmem_limit_bytes=4 * 1024 * 1024)


def roll(value, shift, axis):
    size = value.shape[axis]
    shift = shift % size
    return value if shift == 0 else pltpu.roll(value, shift, axis)


def parity():
    return lax.rem(lax.axis_index("bx"), 2) == 1


def moving(axis, sign):
    return [q for q in range(POPS) if VELOCITY[q][axis] == sign]


def lane_of(shape):
    return lax.broadcasted_iota(jnp.int32, shape, len(shape) - 1)


def pair_index(low, high, count):
    return low * (2 * count - low - 1) // 2 + (high - low - 1)


def collide(pops, rate, solid):
    rho = functools.reduce(jnp.add, pops)
    flux = []
    for axis in range(3):
        plus = functools.reduce(jnp.add, [pops[q] for q in range(POPS) if VELOCITY[q][axis] > 0])
        minus = functools.reduce(jnp.add, [pops[q] for q in range(POPS) if VELOCITY[q][axis] < 0])
        flux.append(plus - minus)
    base = rho - 1.5 * (flux[0] * flux[0] + flux[1] * flux[1] + flux[2] * flux[2])
    rate_odd = 1.0 / (MAGIC_TRT / (1.0 / rate - 0.5) + 0.5)
    relaxed = [None] * POPS
    rest = pops[0] - rate * (pops[0] - WEIGHTS[0] * base)
    relaxed[0] = jnp.where(solid, pops[0], rest)
    for q in range(1, POPS, 2):
        one, two = pops[q], pops[q + 1]
        speed = None
        for axis in range(3):
            if VELOCITY[q][axis] != 0:
                term = flux[axis] if VELOCITY[q][axis] > 0 else -flux[axis]
                speed = term if speed is None else speed + term
        even = rate * (0.5 * (one + two) - WEIGHTS[q] * (base + 4.5 * speed * speed))
        odd = rate_odd * (0.5 * (one - two) - (3.0 * WEIGHTS[q]) * speed)
        relaxed[q] = jnp.where(solid, two, one - even - odd)
        relaxed[q + 1] = jnp.where(solid, one, two - even + odd)
    return relaxed


def gather_kernel(
    count_x, count_y, depth, owner_in, pops_in, rate_in, solid_in,
    one_ref, two_ref, extra_ref, index_ref,
    owner_ref, pops_ref, rate_ref, solid_ref, sems,
):
    owner_copy = pltpu.make_async_copy(owner_in, owner_ref, sems.at[0])
    pops_copy = pltpu.make_async_copy(pops_in, pops_ref, sems.at[1])
    rate_copy = pltpu.make_async_copy(rate_in, rate_ref, sems.at[2])
    solid_copy = pltpu.make_async_copy(solid_in, solid_ref, sems.at[3])
    owner_copy.start()
    pops_copy.start()
    rate_copy.start()
    solid_copy.start()
    owner_copy.wait()
    my_x, my_y = lax.axis_index("bx"), lax.axis_index("by")
    myself = my_x * count_y + my_y
    odd = lax.rem(my_x, 2)
    found, level = {}, {}
    for offset in (-1, 0, 1):
        place = my_x + offset
        inside = (place >= 0) & (place < count_x)
        start = jnp.clip(place, 0, count_x - 1) * (count_y * depth)
        for layer in range(depth):
            shift = lax.rem(owner_ref[start + layer], count_y)
            row = lax.rem(my_y - shift + count_y, count_y)
            hit = (owner_ref[start + row * depth + layer] == myself) & inside
            found[offset, layer] = hit.astype(jnp.int32)
            level[offset, layer] = row * depth + layer
    slots = {}
    before = jnp.int32(0)
    for offset in (-1, 0, 1):
        for layer in range(depth):
            slot = before
            for other in range(depth):
                if other != layer:
                    slot = slot + found[offset, other] * (level[offset, other] < level[offset, layer]).astype(jnp.int32)
            slots[offset, layer] = jnp.minimum(slot, pops_ref.shape[0] - 1)
        for layer in range(depth):
            before = before + found[offset, layer]
    start = my_x * (count_y * depth)
    shift0 = lax.rem(owner_ref[start], count_y)
    shift1 = lax.rem(owner_ref[start + 1], count_y)
    low, high = jnp.minimum(shift0, shift1), jnp.maximum(shift0, shift1)
    index_ref[0] = pair_index(low, high, count_y)
    rate_copy.wait()
    solid_copy.wait()
    narrow = lane_of((1, LANES)) < 64
    for tile in range(TILES):
        flags = jnp.where(solid_ref[:, tile * LANES:(tile + 1) * LANES] == 1, 1.0, 0.0)
        lower, upper = flags[0:1, :], flags[1:2, :]
        extra_ref[pl.ds(2 * tile, 1), :] = jnp.where(narrow, lower, roll(upper, 64, 1))
        extra_ref[pl.ds(2 * tile + 1, 1), :] = jnp.where(narrow, roll(lower, 64, 1), upper)
    extra_ref[pl.ds(EDGE, EDGE), :] = jnp.where(lane_of((EDGE, LANES)) < 64, rate_ref[0], rate_ref[1])
    pops_copy.wait()
    for layer in range(depth):
        left, right = slots[-1, layer], slots[1, layer]
        one = jnp.where(odd == 1, left, right)
        two = jnp.where(odd == 1, right, left)
        for ref, slot in ((one_ref, one), (two_ref, two)):
            for tile in range(TILES):
                ref[pl.ds(layer * ROWS + tile * POPS, POPS), :] = pops_ref[slot, :, tile * LANES:(tile + 1) * LANES]


def flags_kernel(count_y, depth, owner_ref, flags_ref):
    my_x, my_y = lax.axis_index("bx"), lax.axis_index("by")
    owner = owner_ref[...]
    level = lax.broadcasted_iota(jnp.int32, owner.shape, 0) * LANES + lane_of(owner.shape)
    start = my_x * (count_y * depth)
    here = level - start

    def total(mask, value):
        picked = jnp.where(mask, value, 0).astype(jnp.float32)
        return jnp.sum(jnp.sum(picked, axis=0, keepdims=True), axis=1, keepdims=True)

    hops, rows = [], []
    for layer in range(2):
        shift = total(here == layer, lax.rem(owner, count_y))
        hops.append((jnp.minimum(shift, count_y - shift), shift))
        column = (here >= 0) & (here < count_y * depth) & (lax.rem(level, depth) == layer)
        hit = column & (lax.rem(owner, count_y) == my_y)
        source = total(hit, lax.div(owner, count_y) - my_x)
        place = total(hit, level)
        slot = total((owner == my_x * count_y + my_y) & (level.astype(jnp.float32) < place), 1)
        rows.append((source, slot))
    (hops0, shift0), (hops1, shift1) = hops
    swapped = (hops1 > hops0) | ((hops1 == hops0) & (shift1 < shift0))
    values = [jnp.where(swapped, 1.0, 0.0)] + [row[k] for k in range(2) for row in rows]
    for k, value in enumerate(values):
        flags_ref[pl.ds(k, 1), :] = jnp.broadcast_to(value, (1, LANES))


def select_kernel(flags_ref, pops_ref, two_ref, one_ref, near_ref, far_ref):
    flags = [flags_ref[pl.ds(k, 1), :] for k in range(5)]
    swapped = flags[0] > 0.5
    partner = jnp.where(parity(), -1.0, 1.0)
    for tile in range(TILES):
        blocks = []
        for layer in range(2):
            source, slot = flags[1 + layer], flags[3 + layer]
            part = pl.ds(layer * ROWS + tile * POPS, POPS)
            block = jnp.where(source == partner, one_ref[part, :], two_ref[part, :])
            for k in range(pops_ref.shape[0]):
                keep = pops_ref[k, :, tile * LANES:(tile + 1) * LANES]
                block = jnp.where((source == 0.0) & (slot == k), keep, block)
            blocks.append(block)
        far_ref[pl.ds(tile * POPS, POPS), :] = jnp.where(swapped, blocks[1], blocks[0])
        near_ref[pl.ds(tile * POPS, POPS), :] = jnp.where(swapped, blocks[0], blocks[1])


def collide_kernel(extra_ref, flags_ref, near_ref, far_ref, state_ref, down_ref, up_ref):
    swapped = flags_ref[pl.ds(0, 1), :] > 0.5
    wide = lane_of((POPS, LANES)) < 64
    for tile in range(TILES):
        part = pl.ds(tile * POPS, POPS)
        far, near = far_ref[part, :], near_ref[part, :]
        lower = jnp.where(swapped, near, far)
        upper = jnp.where(swapped, far, near)
        state_ref[pl.ds(2 * tile, POPS, stride=EDGE), :] = jnp.where(wide, lower, roll(upper, 64, 1))
        state_ref[pl.ds(2 * tile + 1, POPS, stride=EDGE), :] = jnp.where(wide, roll(lower, 64, 1), upper)
    marks, rate = extra_ref[pl.ds(0, EDGE), :], extra_ref[pl.ds(EDGE, EDGE), :]
    relaxed = collide([state_ref[pl.ds(q * EDGE, EDGE), :] for q in range(POPS)], rate, marks > 0.5)
    values = relaxed + [marks, rate]
    for channel, value in enumerate(values):
        state_ref[pl.ds(channel * EDGE, EDGE), :] = value
    part = lane_of((EDGE, LANES)) // 8
    for ref, beside, second, sign in ((down_ref, 0, 1, -1), (up_ref, EDGE - 1, EDGE - 2, 1)):
        slots = [(channel, beside) for channel in range(CHANNELS)] + [(q, second) for q in moving(1, sign)]
        for group in range(GROUPS):
            packed = None
            for k, (channel, row) in enumerate(slots[8 * group:8 * group + 8]):
                for layer in range(2):
                    moved = roll(values[channel], (2 * k + layer) * 8 - (layer * 64 + row * 8), 1)
                    packed = moved if packed is None else jnp.where(part == 2 * k + layer, moved, packed)
            ref[pl.ds(group * EDGE, EDGE), :] = packed


def widen_kernel(state_ref, below_ref, above_ref, wide_ref, one_ref, two_ref):
    odd = parity()
    part = lane_of((EDGE, LANES)) // 8
    extras = ((below_ref, 3, 2, moving(1, 1)), (above_ref, 12, 13, moving(1, -1)))
    for channel in range(CHANNELS):
        value = state_ref[pl.ds(channel * EDGE, EDGE), :]
        for layer in range(2):
            field = roll(value, 32 - 64 * layer, 1)
            for ref, beside, second, inward in extras:
                slots = [(channel, beside)]
                if channel in inward:
                    slots.append((CHANNELS + inward.index(channel), second))
                for slot, place in slots:
                    group, k = divmod(slot, 8)
                    halo = ref[pl.ds(group * EDGE, EDGE), :]
                    field = jnp.where(part == place, roll(halo, place * 8 - (2 * k + layer) * 8, 1), field)
            wide_ref[pl.ds((layer * CHANNELS + channel) * SPAN + 4, EDGE), :] = field
    for layer in range(2):
        base = layer * CHANNELS * SPAN + 4
        left = wide_ref[pl.ds(base, CHANNELS, stride=SPAN), :]
        right = wide_ref[pl.ds(base + EDGE - 1, CHANNELS, stride=SPAN), :]
        one_ref[pl.ds(layer * SLOTS, CHANNELS), :] = jnp.where(odd, left, right)
        two_ref[pl.ds(layer * SLOTS, CHANNELS), :] = jnp.where(odd, right, left)
        for k, (to_left, to_right) in enumerate(zip(moving(0, -1), moving(0, 1))):
            left = wide_ref[pl.ds(base + to_left * SPAN + 1, 1), :]
            right = wide_ref[pl.ds(base + to_right * SPAN + EDGE - 2, 1), :]
            one_ref[pl.ds(layer * SLOTS + CHANNELS + k, 1), :] = jnp.where(odd, left, right)
            two_ref[pl.ds(layer * SLOTS + CHANNELS + k, 1), :] = jnp.where(odd, right, left)


def stream(fields, depth_place):
    moved = [[None] * POPS for _ in fields]
    for q in range(POPS):
        step_x, step_y, step_z = VELOCITY[q]
        for layer in range(2):
            value = roll(fields[layer][q], 8 * step_y + step_z, 1)
            if step_z != 0:
                outer = roll(fields[1 - layer][q], 8 * step_y - 7 * step_z, 1)
                value = jnp.where(depth_place == (0 if step_z > 0 else 7), outer, value)
            moved[layer][q] = roll(value, step_x, 0)
    return moved


def finish_kernel(wide_ref, two_ref, one_ref, out_ref, halo_ref, last_ref):
    odd = parity()
    place = lane_of((SPAN, LANES)) % 8
    row = lax.broadcasted_iota(jnp.int32, (SPAN, LANES), 0)
    own = (row >= 4) & (row < 4 + EDGE)
    for layer in range(2):
        base = layer * CHANNELS * SPAN
        one, two = one_ref[pl.ds(layer * SLOTS, CHANNELS), :], two_ref[pl.ds(layer * SLOTS, CHANNELS), :]
        halo_ref[pl.ds(base + 3, CHANNELS, stride=SPAN), :] = jnp.where(odd, one, two)
        halo_ref[pl.ds(base + 4 + EDGE, CHANNELS, stride=SPAN), :] = jnp.where(odd, two, one)
        for k, (to_left, to_right) in enumerate(zip(moving(0, -1), moving(0, 1))):
            second = pl.ds(layer * SLOTS + CHANNELS + k, 1)
            one, two = one_ref[second, :], two_ref[second, :]
            halo_ref[pl.ds(base + to_right * SPAN + 2, 1), :] = jnp.where(odd, one, two)
            halo_ref[pl.ds(base + to_left * SPAN + 5 + EDGE, 1), :] = jnp.where(odd, two, one)
    fields = [[None] * CHANNELS for _ in range(2)]
    for layer in range(2):
        for channel in range(CHANNELS):
            part = pl.ds((layer * CHANNELS + channel) * SPAN, SPAN)
            fields[layer][channel] = jnp.where(own, wide_ref[part, :], halo_ref[part, :])
    moved = stream([field[:POPS] for field in fields], place)
    relaxed = [collide(moved[layer], fields[layer][RATE], fields[layer][SOLID] > 0.5) for layer in range(2)]
    final = stream(relaxed, place)
    half = lane_of((POPS, LANES)) < 64
    for layer in range(2):
        for q in range(POPS):
            last_ref[layer, pl.ds(q * SPAN, SPAN), :] = final[layer][q]
        for tile in range(TILES):
            even = last_ref[layer, pl.ds(2 * tile + 4, POPS, stride=SPAN), :]
            odd = last_ref[layer, pl.ds(2 * tile + 5, POPS, stride=SPAN), :]
            out_ref[pl.ds(2 * tile + layer, POPS, stride=2 * TILES), :] = jnp.where(half, roll(even, -32, 1), roll(odd, 32, 1))


def shape_of(*dims, dtype=jnp.float32):
    return jax.ShapeDtypeStruct(dims, dtype)


def local(pops_old, old_owner, relax, solid_mask):
    count_x, count_y = lax.axis_size("bx"), lax.axis_size("by")
    depth = relax.shape[0]
    inside = [pair for k in range(0, count_x, 2) for pair in ((k, k + 1), (k + 1, k))]
    across = [
        pair for k in range(1, count_x, 2) for pair in ((k, (k + 1) % count_x), ((k + 1) % count_x, k))
    ]
    up = [(k, (k + 1) % count_y) for k in range(count_y)]
    down = [(k, (k - 1) % count_y) for k in range(count_y)]

    one, two, extra, index = pl.pallas_call(
        functools.partial(gather_kernel, count_x, count_y, depth),
        out_shape=[shape_of(depth * ROWS, LANES)] * 2
        + [shape_of(2 * EDGE, LANES), shape_of(1, dtype=jnp.int32)],
        in_specs=[HBM] * 4,
        out_specs=[VMEM] * 3 + [SMEM],
        scratch_shapes=[
            pltpu.SMEM(old_owner.shape, jnp.int32),
            pltpu.VMEM(pops_old.shape, jnp.float32),
            pltpu.SMEM(relax.shape, jnp.float32),
            pltpu.VMEM(solid_mask.shape, jnp.int32),
            pltpu.SemaphoreType.DMA((4,)),
        ],
        name="gather_blocks",
    )(old_owner, pops_old, relax, solid_mask)
    two = lax.ppermute(two, "bx", across)
    one = lax.ppermute(one, "bx", inside)
    flags = pl.pallas_call(
        functools.partial(flags_kernel, count_y, depth),
        out_shape=shape_of(EDGE, LANES),
        in_specs=[VMEM],
        out_specs=VMEM,
        compiler_params=SMALL,
        name="flags",
    )(old_owner.reshape(-1, LANES))
    near, far = pl.pallas_call(
        select_kernel,
        out_shape=[shape_of(ROWS, LANES)] * 2,
        in_specs=[VMEM] * 4,
        out_specs=[VMEM] * 2,
        compiler_params=SMALL,
        name="select_blocks",
    )(flags, pops_old, two, one)

    def hops(shift):
        return min(shift % count_y, -shift % count_y)

    def shifted(block, shift):
        if shift % count_y == 0:
            return block
        return lax.ppermute(block, "by", [((k + shift) % count_y, k) for k in range(count_y)])

    def branch(low, high):
        first, second = (high, low) if hops(high) > hops(low) else (low, high)
        return lambda near, far: (shifted(near, second), shifted(far, first))

    pairs = [(low, high) for low in range(count_y) for high in range(low + 1, count_y)]
    near, far = lax.switch(index[0], [branch(*pair) for pair in pairs], near, far)

    state, to_below, to_above = pl.pallas_call(
        collide_kernel,
        out_shape=[shape_of(CHANNELS * EDGE, LANES)] + [shape_of(GROUPS * EDGE, LANES)] * 2,
        in_specs=[VMEM] * 4,
        out_specs=[VMEM] * 3,
        compiler_params=SMALL,
        name="collide_first",
    )(extra, flags, near, far)
    below = lax.ppermute(to_above, "by", up)
    above = lax.ppermute(to_below, "by", down)
    wide, one, two = pl.pallas_call(
        widen_kernel,
        out_shape=[shape_of(2 * CHANNELS * SPAN, LANES)] + [shape_of(2 * SLOTS, LANES)] * 2,
        in_specs=[VMEM] * 3,
        out_specs=[VMEM] * 3,
        compiler_params=SMALL,
        name="widen_pack",
    )(state, below, above)
    two = lax.ppermute(two, "bx", across)
    one = lax.ppermute(one, "bx", inside)
    rows = pl.pallas_call(
        finish_kernel,
        out_shape=shape_of(POPS * TILES * depth, LANES),
        in_specs=[VMEM] * 3,
        out_specs=VMEM,
        scratch_shapes=[
            pltpu.VMEM((2 * CHANNELS * SPAN, LANES), jnp.float32),
            pltpu.VMEM((2, POPS * SPAN, LANES), jnp.float32),
        ],
        compiler_params=SMALL,
        name="stream_collide_stream",
    )(wide, two, one)
    return (
        rows.reshape(POPS, TILES, depth, LANES).transpose(2, 0, 1, 3).reshape(depth, POPS, TILES * LANES)
    )


def solution(mesh):
    return jax.shard_map(
        local,
        mesh=mesh,
        in_specs=(P(("bx", "by"), None, None), P(), P(("bx", "by")), P(("bx", "by"), None)),
        out_specs=P(("bx", "by"), None, None),
        check_vma=False,
    )
```

```python
import functools

import jax
import jax.numpy as jnp
import numpy as np
from jax import lax
from jax.experimental import pallas as pl
from jax.experimental.pallas import tpu as pltpu
from jax.sharding import PartitionSpec as P

EDGE = 8
POPS = 19
TILES = 4
LANES = 128
ROWS = POPS * TILES
CHANNELS = POPS + 2
SOLID = POPS
RATE = POPS + 1
SPAN = 16
INWARD = 5
SLOTS = CHANNELS + INWARD
GROUPS = (SLOTS + 7) // 8

VELOCITY = (
    (0, 0, 0), (1, 0, 0), (-1, 0, 0), (0, 1, 0), (0, -1, 0), (0, 0, 1), (0, 0, -1),
    (1, 1, 0), (-1, -1, 0), (1, -1, 0), (-1, 1, 0), (1, 0, 1), (-1, 0, -1), (1, 0, -1),
    (-1, 0, 1), (0, 1, 1), (0, -1, -1), (0, 1, -1), (0, -1, 1),
)
WEIGHTS = (1.0 / 3.0,) + (1.0 / 18.0,) * 6 + (1.0 / 36.0,) * 12
MAGIC_TRT = 0.1875

VMEM = pl.BlockSpec(memory_space=pltpu.VMEM)
SMEM = pl.BlockSpec(memory_space=pltpu.SMEM)
HBM = pl.BlockSpec(memory_space=pltpu.HBM)
SMALL = pltpu.CompilerParams(vmem_limit_bytes=4 * 1024 * 1024)


def roll(value, shift, axis):
    size = value.shape[axis]
    shift = shift % size
    return value if shift == 0 else pltpu.roll(value, shift, axis)


def parity():
    return lax.rem(lax.axis_index("bx"), 2) == 1


def moving(axis, sign):
    return [q for q in range(POPS) if VELOCITY[q][axis] == sign]


def lane_of(shape):
    return lax.broadcasted_iota(jnp.int32, shape, len(shape) - 1)


def pair_index(low, high, count):
    return low * (2 * count - low - 1) // 2 + (high - low - 1)


def collide(pops, rate, solid):
    rho = functools.reduce(jnp.add, pops)
    flux = []
    for axis in range(3):
        plus = functools.reduce(jnp.add, [pops[q] for q in range(POPS) if VELOCITY[q][axis] > 0])
        minus = functools.reduce(jnp.add, [pops[q] for q in range(POPS) if VELOCITY[q][axis] < 0])
        flux.append(plus - minus)
    base = rho - 1.5 * (flux[0] * flux[0] + flux[1] * flux[1] + flux[2] * flux[2])
    rate_odd = 1.0 / (MAGIC_TRT / (1.0 / rate - 0.5) + 0.5)
    relaxed = [None] * POPS
    rest = pops[0] - rate * (pops[0] - WEIGHTS[0] * base)
    relaxed[0] = jnp.where(solid, pops[0], rest)
    for q in range(1, POPS, 2):
        one, two = pops[q], pops[q + 1]
        speed = None
        for axis in range(3):
            if VELOCITY[q][axis] != 0:
                term = flux[axis] if VELOCITY[q][axis] > 0 else -flux[axis]
                speed = term if speed is None else speed + term
        even = rate * (0.5 * (one + two) - WEIGHTS[q] * (base + 4.5 * speed * speed))
        odd = rate_odd * (0.5 * (one - two) - (3.0 * WEIGHTS[q]) * speed)
        relaxed[q] = jnp.where(solid, two, one - even - odd)
        relaxed[q + 1] = jnp.where(solid, one, two - even + odd)
    return relaxed


def gather_kernel(
    count_x, count_y, depth, owner_in, pops_in, rate_in, solid_in,
    one_ref, two_ref, extra_ref, index_ref,
    owner_ref, pops_ref, rate_ref, solid_ref, sems,
):
    owner_copy = pltpu.make_async_copy(owner_in, owner_ref, sems.at[0])
    pops_copy = pltpu.make_async_copy(pops_in, pops_ref, sems.at[1])
    rate_copy = pltpu.make_async_copy(rate_in, rate_ref, sems.at[2])
    solid_copy = pltpu.make_async_copy(solid_in, solid_ref, sems.at[3])
    owner_copy.start()
    pops_copy.start()
    rate_copy.start()
    solid_copy.start()
    owner_copy.wait()
    my_x, my_y = lax.axis_index("bx"), lax.axis_index("by")
    myself = my_x * count_y + my_y
    odd = lax.rem(my_x, 2)
    found, level = {}, {}
    for offset in (-1, 0, 1):
        place = my_x + offset
        inside = (place >= 0) & (place < count_x)
        start = jnp.clip(place, 0, count_x - 1) * (count_y * depth)
        for layer in range(depth):
            shift = lax.rem(owner_ref[start + layer], count_y)
            row = lax.rem(my_y - shift + count_y, count_y)
            hit = (owner_ref[start + row * depth + layer] == myself) & inside
            found[offset, layer] = hit.astype(jnp.int32)
            level[offset, layer] = row * depth + layer
    slots = {}
    before = jnp.int32(0)
    for offset in (-1, 0, 1):
        for layer in range(depth):
            slot = before
            for other in range(depth):
                if other != layer:
                    slot = slot + found[offset, other] * (level[offset, other] < level[offset, layer]).astype(jnp.int32)
            slots[offset, layer] = jnp.minimum(slot, pops_ref.shape[0] - 1)
        for layer in range(depth):
            before = before + found[offset, layer]
    start = my_x * (count_y * depth)
    shift0 = lax.rem(owner_ref[start], count_y)
    shift1 = lax.rem(owner_ref[start + 1], count_y)
    low, high = jnp.minimum(shift0, shift1), jnp.maximum(shift0, shift1)
    index_ref[0] = pair_index(low, high, count_y)
    rate_copy.wait()
    solid_copy.wait()
    narrow = lane_of((1, LANES)) < 64
    for tile in range(TILES):
        flags = jnp.where(solid_ref[:, tile * LANES:(tile + 1) * LANES] == 1, 1.0, 0.0)
        lower, upper = flags[0:1, :], flags[1:2, :]
        extra_ref[pl.ds(2 * tile, 1), :] = jnp.where(narrow, lower, roll(upper, 64, 1))
        extra_ref[pl.ds(2 * tile + 1, 1), :] = jnp.where(narrow, roll(lower, 64, 1), upper)
    extra_ref[pl.ds(EDGE, EDGE), :] = jnp.where(lane_of((EDGE, LANES)) < 64, rate_ref[0], rate_ref[1])
    pops_copy.wait()
    for layer in range(depth):
        left, right = slots[-1, layer], slots[1, layer]
        one = jnp.where(odd == 1, left, right)
        two = jnp.where(odd == 1, right, left)
        for ref, slot in ((one_ref, one), (two_ref, two)):
            for tile in range(TILES):
                ref[pl.ds(layer * ROWS + tile * POPS, POPS), :] = pops_ref[slot, :, tile * LANES:(tile + 1) * LANES]


def flags_kernel(count_y, depth, owner_ref, flags_ref):
    my_x, my_y = lax.axis_index("bx"), lax.axis_index("by")
    owner = owner_ref[...]
    level = lax.broadcasted_iota(jnp.int32, owner.shape, 0) * LANES + lane_of(owner.shape)
    start = my_x * (count_y * depth)
    here = level - start

    def total(mask, value):
        picked = jnp.where(mask, value, 0).astype(jnp.float32)
        return jnp.sum(jnp.sum(picked, axis=0, keepdims=True), axis=1, keepdims=True)

    hops, rows = [], []
    for layer in range(2):
        shift = total(here == layer, lax.rem(owner, count_y))
        hops.append((jnp.minimum(shift, count_y - shift), shift))
        column = (here >= 0) & (here < count_y * depth) & (lax.rem(level, depth) == layer)
        hit = column & (lax.rem(owner, count_y) == my_y)
        source = total(hit, lax.div(owner, count_y) - my_x)
        place = total(hit, level)
        slot = total((owner == my_x * count_y + my_y) & (level.astype(jnp.float32) < place), 1)
        rows.append((source, slot))
    (hops0, shift0), (hops1, shift1) = hops
    swapped = (hops1 > hops0) | ((hops1 == hops0) & (shift1 < shift0))
    values = [jnp.where(swapped, 1.0, 0.0)] + [row[k] for k in range(2) for row in rows]
    for k, value in enumerate(values):
        flags_ref[pl.ds(k, 1), :] = jnp.broadcast_to(value, (1, LANES))


def select_kernel(flags_ref, pops_ref, two_ref, one_ref, near_ref, far_ref):
    flags = [flags_ref[pl.ds(k, 1), :] for k in range(5)]
    swapped = flags[0] > 0.5
    partner = jnp.where(parity(), -1.0, 1.0)
    for tile in range(TILES):
        blocks = []
        for layer in range(2):
            source, slot = flags[1 + layer], flags[3 + layer]
            part = pl.ds(layer * ROWS + tile * POPS, POPS)
            block = jnp.where(source == partner, one_ref[part, :], two_ref[part, :])
            for k in range(pops_ref.shape[0]):
                keep = pops_ref[k, :, tile * LANES:(tile + 1) * LANES]
                block = jnp.where((source == 0.0) & (slot == k), keep, block)
            blocks.append(block)
        far_ref[pl.ds(tile * POPS, POPS), :] = jnp.where(swapped, blocks[1], blocks[0])
        near_ref[pl.ds(tile * POPS, POPS), :] = jnp.where(swapped, blocks[0], blocks[1])


def collide_kernel(extra_ref, flags_ref, near_ref, far_ref, state_ref, down_ref, up_ref):
    swapped = flags_ref[pl.ds(0, 1), :] > 0.5
    wide = lane_of((POPS, LANES)) < 64
    for tile in range(TILES):
        part = pl.ds(tile * POPS, POPS)
        far, near = far_ref[part, :], near_ref[part, :]
        lower = jnp.where(swapped, near, far)
        upper = jnp.where(swapped, far, near)
        state_ref[pl.ds(2 * tile, POPS, stride=EDGE), :] = jnp.where(wide, lower, roll(upper, 64, 1))
        state_ref[pl.ds(2 * tile + 1, POPS, stride=EDGE), :] = jnp.where(wide, roll(lower, 64, 1), upper)
    marks, rate = extra_ref[pl.ds(0, EDGE), :], extra_ref[pl.ds(EDGE, EDGE), :]
    relaxed = collide([state_ref[pl.ds(q * EDGE, EDGE), :] for q in range(POPS)], rate, marks > 0.5)
    values = relaxed + [marks, rate]
    for channel, value in enumerate(values):
        state_ref[pl.ds(channel * EDGE, EDGE), :] = value
    part = lane_of((EDGE, LANES)) // 8
    for ref, beside, second, sign in ((down_ref, 0, 1, -1), (up_ref, EDGE - 1, EDGE - 2, 1)):
        slots = [(channel, beside) for channel in range(CHANNELS)] + [(q, second) for q in moving(1, sign)]
        for group in range(GROUPS):
            packed = None
            for k, (channel, row) in enumerate(slots[8 * group:8 * group + 8]):
                for layer in range(2):
                    moved = roll(values[channel], (2 * k + layer) * 8 - (layer * 64 + row * 8), 1)
                    packed = moved if packed is None else jnp.where(part == 2 * k + layer, moved, packed)
            ref[pl.ds(group * EDGE, EDGE), :] = packed


def widen_kernel(state_ref, below_ref, above_ref, wide_ref, one_ref, two_ref):
    odd = parity()
    part = lane_of((EDGE, LANES)) // 8
    extras = ((below_ref, 3, 2, moving(1, 1)), (above_ref, 12, 13, moving(1, -1)))
    for channel in range(CHANNELS):
        value = state_ref[pl.ds(channel * EDGE, EDGE), :]
        for layer in range(2):
            field = roll(value, 32 - 64 * layer, 1)
            for ref, beside, second, inward in extras:
                slots = [(channel, beside)]
                if channel in inward:
                    slots.append((CHANNELS + inward.index(channel), second))
                for slot, place in slots:
                    group, k = divmod(slot, 8)
                    halo = ref[pl.ds(group * EDGE, EDGE), :]
                    field = jnp.where(part == place, roll(halo, place * 8 - (2 * k + layer) * 8, 1), field)
            wide_ref[pl.ds((layer * CHANNELS + channel) * SPAN + 4, EDGE), :] = field
    for layer in range(2):
        base = layer * CHANNELS * SPAN + 4
        left = wide_ref[pl.ds(base, CHANNELS, stride=SPAN), :]
        right = wide_ref[pl.ds(base + EDGE - 1, CHANNELS, stride=SPAN), :]
        one_ref[pl.ds(layer * SLOTS, CHANNELS), :] = jnp.where(odd, left, right)
        two_ref[pl.ds(layer * SLOTS, CHANNELS), :] = jnp.where(odd, right, left)
        for k, (to_left, to_right) in enumerate(zip(moving(0, -1), moving(0, 1))):
            left = wide_ref[pl.ds(base + to_left * SPAN + 1, 1), :]
            right = wide_ref[pl.ds(base + to_right * SPAN + EDGE - 2, 1), :]
            one_ref[pl.ds(layer * SLOTS + CHANNELS + k, 1), :] = jnp.where(odd, left, right)
            two_ref[pl.ds(layer * SLOTS + CHANNELS + k, 1), :] = jnp.where(odd, right, left)


def stream(fields, depth_place):
    moved = [[None] * POPS for _ in fields]
    for q in range(POPS):
        step_x, step_y, step_z = VELOCITY[q]
        for layer in range(2):
            value = roll(fields[layer][q], 8 * step_y + step_z, 1)
            if step_z != 0:
                outer = roll(fields[1 - layer][q], 8 * step_y - 7 * step_z, 1)
                value = jnp.where(depth_place == (0 if step_z > 0 else 7), outer, value)
            moved[layer][q] = roll(value, step_x, 0)
    return moved


def finish_kernel(wide_ref, two_ref, one_ref, out_ref, halo_ref, last_ref):
    odd = parity()
    place = lane_of((SPAN, LANES)) % 8
    row = lax.broadcasted_iota(jnp.int32, (SPAN, LANES), 0)
    own = (row >= 4) & (row < 4 + EDGE)
    for layer in range(2):
        base = layer * CHANNELS * SPAN
        one, two = one_ref[pl.ds(layer * SLOTS, CHANNELS), :], two_ref[pl.ds(layer * SLOTS, CHANNELS), :]
        halo_ref[pl.ds(base + 3, CHANNELS, stride=SPAN), :] = jnp.where(odd, one, two)
        halo_ref[pl.ds(base + 4 + EDGE, CHANNELS, stride=SPAN), :] = jnp.where(odd, two, one)
        for k, (to_left, to_right) in enumerate(zip(moving(0, -1), moving(0, 1))):
            second = pl.ds(layer * SLOTS + CHANNELS + k, 1)
            one, two = one_ref[second, :], two_ref[second, :]
            halo_ref[pl.ds(base + to_right * SPAN + 2, 1), :] = jnp.where(odd, one, two)
            halo_ref[pl.ds(base + to_left * SPAN + 5 + EDGE, 1), :] = jnp.where(odd, two, one)
    fields = [[None] * CHANNELS for _ in range(2)]
    for layer in range(2):
        for channel in range(CHANNELS):
            part = pl.ds((layer * CHANNELS + channel) * SPAN, SPAN)
            fields[layer][channel] = jnp.where(own, wide_ref[part, :], halo_ref[part, :])
    moved = stream([field[:POPS] for field in fields], place)
    relaxed = [collide(moved[layer], fields[layer][RATE], fields[layer][SOLID] > 0.5) for layer in range(2)]
    final = stream(relaxed, place)
    half = lane_of((POPS, LANES)) < 64
    for layer in range(2):
        for q in range(POPS):
            last_ref[layer, pl.ds(q * SPAN, SPAN), :] = final[layer][q]
        for tile in range(TILES):
            even = last_ref[layer, pl.ds(2 * tile + 4, POPS, stride=SPAN), :]
            odd = last_ref[layer, pl.ds(2 * tile + 5, POPS, stride=SPAN), :]
            out_ref[pl.ds(2 * tile + layer, POPS, stride=2 * TILES), :] = jnp.where(half, roll(even, -32, 1), roll(odd, 32, 1))


def shape_of(*dims, dtype=jnp.float32):
    return jax.ShapeDtypeStruct(dims, dtype)


def local(pops_old, old_owner, relax, solid_mask):
    count_x, count_y = lax.axis_size("bx"), lax.axis_size("by")
    depth = relax.shape[0]
    inside = [pair for k in range(0, count_x, 2) for pair in ((k, k + 1), (k + 1, k))]
    across = [pair for k in range(1, count_x - 1, 2) for pair in ((k, k + 1), (k + 1, k))]
    around = across + [(count_x - 1, 0), (0, count_x - 1)]
    up = [(k, (k + 1) % count_y) for k in range(count_y)]
    down = [(k, (k - 1) % count_y) for k in range(count_y)]

    one, two, extra, index = pl.pallas_call(
        functools.partial(gather_kernel, count_x, count_y, depth),
        out_shape=[shape_of(depth * ROWS, LANES)] * 2
        + [shape_of(2 * EDGE, LANES), shape_of(1, dtype=jnp.int32)],
        in_specs=[HBM] * 4,
        out_specs=[VMEM] * 3 + [SMEM],
        scratch_shapes=[
            pltpu.SMEM(old_owner.shape, jnp.int32),
            pltpu.VMEM(pops_old.shape, jnp.float32),
            pltpu.SMEM(relax.shape, jnp.float32),
            pltpu.VMEM(solid_mask.shape, jnp.int32),
            pltpu.SemaphoreType.DMA((4,)),
        ],
        name="gather_blocks",
    )(old_owner, pops_old, relax, solid_mask)
    two = lax.ppermute(two, "bx", across)
    one = lax.ppermute(one, "bx", inside)
    flags = pl.pallas_call(
        functools.partial(flags_kernel, count_y, depth),
        out_shape=shape_of(EDGE, LANES),
        in_specs=[VMEM],
        out_specs=VMEM,
        compiler_params=SMALL,
        name="flags",
    )(old_owner.reshape(-1, LANES))
    near, far = pl.pallas_call(
        select_kernel,
        out_shape=[shape_of(ROWS, LANES)] * 2,
        in_specs=[VMEM] * 4,
        out_specs=[VMEM] * 2,
        compiler_params=SMALL,
        name="select_blocks",
    )(flags, pops_old, two, one)

    def hops(shift):
        return min(shift % count_y, -shift % count_y)

    def shifted(block, shift):
        if shift % count_y == 0:
            return block
        return lax.ppermute(block, "by", [((k + shift) % count_y, k) for k in range(count_y)])

    def branch(low, high):
        first, second = (high, low) if hops(high) > hops(low) else (low, high)
        return lambda near, far: (shifted(near, second), shifted(far, first))

    pairs = [(low, high) for low in range(count_y) for high in range(low + 1, count_y)]
    near, far = lax.switch(index[0], [branch(*pair) for pair in pairs], near, far)

    state, to_below, to_above = pl.pallas_call(
        collide_kernel,
        out_shape=[shape_of(CHANNELS * EDGE, LANES)] + [shape_of(GROUPS * EDGE, LANES)] * 2,
        in_specs=[VMEM] * 4,
        out_specs=[VMEM] * 3,
        compiler_params=SMALL,
        name="collide_first",
    )(extra, flags, near, far)
    below = lax.ppermute(to_above, "by", up)
    above = lax.ppermute(to_below, "by", down)
    wide, one, two = pl.pallas_call(
        widen_kernel,
        out_shape=[shape_of(2 * CHANNELS * SPAN, LANES)] + [shape_of(2 * SLOTS, LANES)] * 2,
        in_specs=[VMEM] * 3,
        out_specs=[VMEM] * 3,
        compiler_params=SMALL,
        name="widen_pack",
    )(state, below, above)
    two = lax.ppermute(two, "bx", around)
    one = lax.ppermute(one, "bx", inside)
    rows = pl.pallas_call(
        finish_kernel,
        out_shape=shape_of(POPS * TILES * depth, LANES),
        in_specs=[VMEM] * 3,
        out_specs=VMEM,
        scratch_shapes=[
            pltpu.VMEM((2 * CHANNELS * SPAN, LANES), jnp.float32),
            pltpu.VMEM((2, POPS * SPAN, LANES), jnp.float32),
        ],
        compiler_params=SMALL,
        name="stream_collide_stream",
    )(wide, two, one)
    return (
        rows.reshape(POPS, TILES, depth, LANES).transpose(2, 0, 1, 3).reshape(depth, POPS, TILES * LANES)
    )


def solution(mesh):
    return jax.shard_map(
        local,
        mesh=mesh,
        in_specs=(P(("bx", "by"), None, None), P(), P(("bx", "by")), P(("bx", "by"), None)),
        out_specs=P(("bx", "by"), None, None),
        check_vma=False,
    )
```

```python
import functools

import jax
import jax.numpy as jnp
import numpy as np
from jax import lax
from jax.experimental import pallas as pl
from jax.experimental.pallas import tpu as pltpu
from jax.sharding import PartitionSpec as P

EDGE = 8
POPS = 19
TILES = 4
LANES = 128
ROWS = POPS * TILES
CHANNELS = POPS + 2
SOLID = POPS
RATE = POPS + 1
SPAN = 16
INWARD = 5
SLOTS = CHANNELS + INWARD
GROUPS = (SLOTS + 7) // 8

VELOCITY = (
    (0, 0, 0), (1, 0, 0), (-1, 0, 0), (0, 1, 0), (0, -1, 0), (0, 0, 1), (0, 0, -1),
    (1, 1, 0), (-1, -1, 0), (1, -1, 0), (-1, 1, 0), (1, 0, 1), (-1, 0, -1), (1, 0, -1),
    (-1, 0, 1), (0, 1, 1), (0, -1, -1), (0, 1, -1), (0, -1, 1),
)
WEIGHTS = (1.0 / 3.0,) + (1.0 / 18.0,) * 6 + (1.0 / 36.0,) * 12
MAGIC_TRT = 0.1875

VMEM = pl.BlockSpec(memory_space=pltpu.VMEM)
SMEM = pl.BlockSpec(memory_space=pltpu.SMEM)
HBM = pl.BlockSpec(memory_space=pltpu.HBM)
SMALL = pltpu.CompilerParams(vmem_limit_bytes=4 * 1024 * 1024)


def roll(value, shift, axis):
    size = value.shape[axis]
    shift = shift % size
    return value if shift == 0 else pltpu.roll(value, shift, axis)


def parity(axis="bx"):
    return lax.rem(lax.axis_index(axis), 2) == 1


def moving(axis, sign):
    return [q for q in range(POPS) if VELOCITY[q][axis] == sign]


def lane_of(shape):
    return lax.broadcasted_iota(jnp.int32, shape, len(shape) - 1)


def pair_index(low, high, count):
    return low * (2 * count - low - 1) // 2 + (high - low - 1)


def collide(pops, rate, solid):
    rho = functools.reduce(jnp.add, pops)
    flux = []
    for axis in range(3):
        plus = functools.reduce(jnp.add, [pops[q] for q in range(POPS) if VELOCITY[q][axis] > 0])
        minus = functools.reduce(jnp.add, [pops[q] for q in range(POPS) if VELOCITY[q][axis] < 0])
        flux.append(plus - minus)
    base = rho - 1.5 * (flux[0] * flux[0] + flux[1] * flux[1] + flux[2] * flux[2])
    rate_odd = 1.0 / (MAGIC_TRT / (1.0 / rate - 0.5) + 0.5)
    relaxed = [None] * POPS
    rest = pops[0] - rate * (pops[0] - WEIGHTS[0] * base)
    relaxed[0] = jnp.where(solid, pops[0], rest)
    for q in range(1, POPS, 2):
        one, two = pops[q], pops[q + 1]
        speed = None
        for axis in range(3):
            if VELOCITY[q][axis] != 0:
                term = flux[axis] if VELOCITY[q][axis] > 0 else -flux[axis]
                speed = term if speed is None else speed + term
        even = rate * (0.5 * (one + two) - WEIGHTS[q] * (base + 4.5 * speed * speed))
        odd = rate_odd * (0.5 * (one - two) - (3.0 * WEIGHTS[q]) * speed)
        relaxed[q] = jnp.where(solid, two, one - even - odd)
        relaxed[q + 1] = jnp.where(solid, one, two - even + odd)
    return relaxed


def gather_kernel(
    count_x, count_y, depth, owner_in, pops_in, rate_in, solid_in,
    one_ref, two_ref, extra_ref, index_ref,
    owner_ref, pops_ref, rate_ref, solid_ref, sems,
):
    owner_copy = pltpu.make_async_copy(owner_in, owner_ref, sems.at[0])
    pops_copy = pltpu.make_async_copy(pops_in, pops_ref, sems.at[1])
    rate_copy = pltpu.make_async_copy(rate_in, rate_ref, sems.at[2])
    solid_copy = pltpu.make_async_copy(solid_in, solid_ref, sems.at[3])
    owner_copy.start()
    pops_copy.start()
    rate_copy.start()
    solid_copy.start()
    owner_copy.wait()
    my_x, my_y = lax.axis_index("bx"), lax.axis_index("by")
    myself = my_x * count_y + my_y
    odd = lax.rem(my_x, 2)
    found, level = {}, {}
    for offset in (-1, 0, 1):
        place = my_x + offset
        inside = (place >= 0) & (place < count_x)
        start = jnp.clip(place, 0, count_x - 1) * (count_y * depth)
        for layer in range(depth):
            shift = lax.rem(owner_ref[start + layer], count_y)
            row = lax.rem(my_y - shift + count_y, count_y)
            hit = (owner_ref[start + row * depth + layer] == myself) & inside
            found[offset, layer] = hit.astype(jnp.int32)
            level[offset, layer] = row * depth + layer
    slots = {}
    before = jnp.int32(0)
    for offset in (-1, 0, 1):
        for layer in range(depth):
            slot = before
            for other in range(depth):
                if other != layer:
                    slot = slot + found[offset, other] * (level[offset, other] < level[offset, layer]).astype(jnp.int32)
            slots[offset, layer] = jnp.minimum(slot, pops_ref.shape[0] - 1)
        for layer in range(depth):
            before = before + found[offset, layer]
    start = my_x * (count_y * depth)
    shift0 = lax.rem(owner_ref[start], count_y)
    shift1 = lax.rem(owner_ref[start + 1], count_y)
    low, high = jnp.minimum(shift0, shift1), jnp.maximum(shift0, shift1)
    index_ref[0] = pair_index(low, high, count_y)
    rate_copy.wait()
    solid_copy.wait()
    narrow = lane_of((1, LANES)) < 64
    for tile in range(TILES):
        flags = jnp.where(solid_ref[:, tile * LANES:(tile + 1) * LANES] == 1, 1.0, 0.0)
        lower, upper = flags[0:1, :], flags[1:2, :]
        extra_ref[pl.ds(2 * tile, 1), :] = jnp.where(narrow, lower, roll(upper, 64, 1))
        extra_ref[pl.ds(2 * tile + 1, 1), :] = jnp.where(narrow, roll(lower, 64, 1), upper)
    extra_ref[pl.ds(EDGE, EDGE), :] = jnp.where(lane_of((EDGE, LANES)) < 64, rate_ref[0], rate_ref[1])
    pops_copy.wait()
    for layer in range(depth):
        left, right = slots[-1, layer], slots[1, layer]
        one = jnp.where(odd == 1, left, right)
        two = jnp.where(odd == 1, right, left)
        for ref, slot in ((one_ref, one), (two_ref, two)):
            for tile in range(TILES):
                ref[pl.ds(layer * ROWS + tile * POPS, POPS), :] = pops_ref[slot, :, tile * LANES:(tile + 1) * LANES]


def flags_kernel(count_y, depth, owner_ref, flags_ref):
    my_x, my_y = lax.axis_index("bx"), lax.axis_index("by")
    owner = owner_ref[...]
    level = lax.broadcasted_iota(jnp.int32, owner.shape, 0) * LANES + lane_of(owner.shape)
    start = my_x * (count_y * depth)
    here = level - start

    def total(mask, value):
        picked = jnp.where(mask, value, 0).astype(jnp.float32)
        return jnp.sum(jnp.sum(picked, axis=0, keepdims=True), axis=1, keepdims=True)

    hops, rows = [], []
    for layer in range(2):
        shift = total(here == layer, lax.rem(owner, count_y))
        hops.append((jnp.minimum(shift, count_y - shift), shift))
        column = (here >= 0) & (here < count_y * depth) & (lax.rem(level, depth) == layer)
        hit = column & (lax.rem(owner, count_y) == my_y)
        source = total(hit, lax.div(owner, count_y) - my_x)
        place = total(hit, level)
        slot = total((owner == my_x * count_y + my_y) & (level.astype(jnp.float32) < place), 1)
        rows.append((source, slot))
    (hops0, shift0), (hops1, shift1) = hops
    swapped = (hops1 > hops0) | ((hops1 == hops0) & (shift1 < shift0))
    values = [jnp.where(swapped, 1.0, 0.0)] + [row[k] for k in range(2) for row in rows]
    for k, value in enumerate(values):
        flags_ref[pl.ds(k, 1), :] = jnp.broadcast_to(value, (1, LANES))


def select_kernel(flags_ref, pops_ref, two_ref, one_ref, near_ref, far_ref):
    flags = [flags_ref[pl.ds(k, 1), :] for k in range(5)]
    swapped = flags[0] > 0.5
    partner = jnp.where(parity(), -1.0, 1.0)
    for tile in range(TILES):
        blocks = []
        for layer in range(2):
            source, slot = flags[1 + layer], flags[3 + layer]
            part = pl.ds(layer * ROWS + tile * POPS, POPS)
            block = jnp.where(source == partner, one_ref[part, :], two_ref[part, :])
            for k in range(pops_ref.shape[0]):
                keep = pops_ref[k, :, tile * LANES:(tile + 1) * LANES]
                block = jnp.where((source == 0.0) & (slot == k), keep, block)
            blocks.append(block)
        far_ref[pl.ds(tile * POPS, POPS), :] = jnp.where(swapped, blocks[1], blocks[0])
        near_ref[pl.ds(tile * POPS, POPS), :] = jnp.where(swapped, blocks[0], blocks[1])


def collide_kernel(extra_ref, flags_ref, near_ref, far_ref, state_ref, first_ref, second_ref):
    swapped = flags_ref[pl.ds(0, 1), :] > 0.5
    wide = lane_of((POPS, LANES)) < 64
    for tile in range(TILES):
        part = pl.ds(tile * POPS, POPS)
        far, near = far_ref[part, :], near_ref[part, :]
        lower = jnp.where(swapped, near, far)
        upper = jnp.where(swapped, far, near)
        state_ref[pl.ds(2 * tile, POPS, stride=EDGE), :] = jnp.where(wide, lower, roll(upper, 64, 1))
        state_ref[pl.ds(2 * tile + 1, POPS, stride=EDGE), :] = jnp.where(wide, roll(lower, 64, 1), upper)
    marks, rate = extra_ref[pl.ds(0, EDGE), :], extra_ref[pl.ds(EDGE, EDGE), :]
    relaxed = collide([state_ref[pl.ds(q * EDGE, EDGE), :] for q in range(POPS)], rate, marks > 0.5)
    values = relaxed + [marks, rate]
    for channel, value in enumerate(values):
        state_ref[pl.ds(channel * EDGE, EDGE), :] = value
    part = lane_of((EDGE, LANES)) // 8
    odd = parity("by")
    for group in range(GROUPS):
        faces = []
        for beside, second, sign in ((0, 1, -1), (EDGE - 1, EDGE - 2, 1)):
            slots = [(channel, beside) for channel in range(CHANNELS)] + [(q, second) for q in moving(1, sign)]
            packed = None
            for k, (channel, row) in enumerate(slots[8 * group:8 * group + 8]):
                for layer in range(2):
                    moved = roll(values[channel], (2 * k + layer) * 8 - (layer * 64 + row * 8), 1)
                    packed = moved if packed is None else jnp.where(part == 2 * k + layer, moved, packed)
            faces.append(packed)
        down, up = faces
        first_ref[pl.ds(group * EDGE, EDGE), :] = jnp.where(odd, down, up)
        second_ref[pl.ds(group * EDGE, EDGE), :] = jnp.where(odd, up, down)


def widen_kernel(state_ref, second_ref, first_ref, wide_ref, one_ref, two_ref):
    odd = parity()
    part = lane_of((EDGE, LANES)) // 8
    first = [first_ref[pl.ds(group * EDGE, EDGE), :] for group in range(GROUPS)]
    second = [second_ref[pl.ds(group * EDGE, EDGE), :] for group in range(GROUPS)]
    odd_row = parity("by")
    below = [jnp.where(odd_row, a, b) for a, b in zip(first, second)]
    above = [jnp.where(odd_row, b, a) for a, b in zip(first, second)]
    extras = ((below, 3, 2, moving(1, 1)), (above, 12, 13, moving(1, -1)))
    for channel in range(CHANNELS):
        value = state_ref[pl.ds(channel * EDGE, EDGE), :]
        for layer in range(2):
            field = roll(value, 32 - 64 * layer, 1)
            for halos, beside, second, inward in extras:
                slots = [(channel, beside)]
                if channel in inward:
                    slots.append((CHANNELS + inward.index(channel), second))
                for slot, place in slots:
                    group, k = divmod(slot, 8)
                    field = jnp.where(part == place, roll(halos[group], place * 8 - (2 * k + layer) * 8, 1), field)
            wide_ref[pl.ds((layer * CHANNELS + channel) * SPAN + 4, EDGE), :] = field
    for layer in range(2):
        base = layer * CHANNELS * SPAN + 4
        left = wide_ref[pl.ds(base, CHANNELS, stride=SPAN), :]
        right = wide_ref[pl.ds(base + EDGE - 1, CHANNELS, stride=SPAN), :]
        one_ref[pl.ds(layer * SLOTS, CHANNELS), :] = jnp.where(odd, left, right)
        two_ref[pl.ds(layer * SLOTS, CHANNELS), :] = jnp.where(odd, right, left)
        for k, (to_left, to_right) in enumerate(zip(moving(0, -1), moving(0, 1))):
            left = wide_ref[pl.ds(base + to_left * SPAN + 1, 1), :]
            right = wide_ref[pl.ds(base + to_right * SPAN + EDGE - 2, 1), :]
            one_ref[pl.ds(layer * SLOTS + CHANNELS + k, 1), :] = jnp.where(odd, left, right)
            two_ref[pl.ds(layer * SLOTS + CHANNELS + k, 1), :] = jnp.where(odd, right, left)


def stream(fields, depth_place):
    moved = [[None] * POPS for _ in fields]
    for q in range(POPS):
        step_x, step_y, step_z = VELOCITY[q]
        for layer in range(2):
            value = roll(fields[layer][q], 8 * step_y + step_z, 1)
            if step_z != 0:
                outer = roll(fields[1 - layer][q], 8 * step_y - 7 * step_z, 1)
                value = jnp.where(depth_place == (0 if step_z > 0 else 7), outer, value)
            moved[layer][q] = roll(value, step_x, 0)
    return moved


def finish_kernel(wide_ref, two_ref, one_ref, out_ref, halo_ref, last_ref):
    odd = parity()
    place = lane_of((SPAN, LANES)) % 8
    row = lax.broadcasted_iota(jnp.int32, (SPAN, LANES), 0)
    own = (row >= 4) & (row < 4 + EDGE)
    for layer in range(2):
        base = layer * CHANNELS * SPAN
        one, two = one_ref[pl.ds(layer * SLOTS, CHANNELS), :], two_ref[pl.ds(layer * SLOTS, CHANNELS), :]
        halo_ref[pl.ds(base + 3, CHANNELS, stride=SPAN), :] = jnp.where(odd, one, two)
        halo_ref[pl.ds(base + 4 + EDGE, CHANNELS, stride=SPAN), :] = jnp.where(odd, two, one)
        for k, (to_left, to_right) in enumerate(zip(moving(0, -1), moving(0, 1))):
            second = pl.ds(layer * SLOTS + CHANNELS + k, 1)
            one, two = one_ref[second, :], two_ref[second, :]
            halo_ref[pl.ds(base + to_right * SPAN + 2, 1), :] = jnp.where(odd, one, two)
            halo_ref[pl.ds(base + to_left * SPAN + 5 + EDGE, 1), :] = jnp.where(odd, two, one)
    fields = [[None] * CHANNELS for _ in range(2)]
    for layer in range(2):
        for channel in range(CHANNELS):
            part = pl.ds((layer * CHANNELS + channel) * SPAN, SPAN)
            fields[layer][channel] = jnp.where(own, wide_ref[part, :], halo_ref[part, :])
    moved = stream([field[:POPS] for field in fields], place)
    relaxed = [collide(moved[layer], fields[layer][RATE], fields[layer][SOLID] > 0.5) for layer in range(2)]
    final = stream(relaxed, place)
    half = lane_of((POPS, LANES)) < 64
    for layer in range(2):
        for q in range(POPS):
            last_ref[layer, pl.ds(q * SPAN, SPAN), :] = final[layer][q]
        for tile in range(TILES):
            even = last_ref[layer, pl.ds(2 * tile + 4, POPS, stride=SPAN), :]
            odd = last_ref[layer, pl.ds(2 * tile + 5, POPS, stride=SPAN), :]
            out_ref[pl.ds(2 * tile + layer, POPS, stride=2 * TILES), :] = jnp.where(half, roll(even, -32, 1), roll(odd, 32, 1))


def shape_of(*dims, dtype=jnp.float32):
    return jax.ShapeDtypeStruct(dims, dtype)


def local(pops_old, old_owner, relax, solid_mask):
    count_x, count_y = lax.axis_size("bx"), lax.axis_size("by")
    depth = relax.shape[0]
    inside = [pair for k in range(0, count_x, 2) for pair in ((k, k + 1), (k + 1, k))]
    across = [pair for k in range(1, count_x - 1, 2) for pair in ((k, k + 1), (k + 1, k))]
    around = across + [(count_x - 1, 0), (0, count_x - 1)]
    lower = [pair for k in range(0, count_y, 2) for pair in ((k, k + 1), (k + 1, k))]
    upper = [
        pair for k in range(1, count_y, 2) for pair in ((k, (k + 1) % count_y), ((k + 1) % count_y, k))
    ]

    one, two, extra, index = pl.pallas_call(
        functools.partial(gather_kernel, count_x, count_y, depth),
        out_shape=[shape_of(depth * ROWS, LANES)] * 2
        + [shape_of(2 * EDGE, LANES), shape_of(1, dtype=jnp.int32)],
        in_specs=[HBM] * 4,
        out_specs=[VMEM] * 3 + [SMEM],
        scratch_shapes=[
            pltpu.SMEM(old_owner.shape, jnp.int32),
            pltpu.VMEM(pops_old.shape, jnp.float32),
            pltpu.SMEM(relax.shape, jnp.float32),
            pltpu.VMEM(solid_mask.shape, jnp.int32),
            pltpu.SemaphoreType.DMA((4,)),
        ],
        name="gather_blocks",
    )(old_owner, pops_old, relax, solid_mask)
    two = lax.ppermute(two, "bx", across)
    one = lax.ppermute(one, "bx", inside)
    flags = pl.pallas_call(
        functools.partial(flags_kernel, count_y, depth),
        out_shape=shape_of(EDGE, LANES),
        in_specs=[VMEM],
        out_specs=VMEM,
        compiler_params=SMALL,
        name="flags",
    )(old_owner.reshape(-1, LANES))
    near, far = pl.pallas_call(
        select_kernel,
        out_shape=[shape_of(ROWS, LANES)] * 2,
        in_specs=[VMEM] * 4,
        out_specs=[VMEM] * 2,
        compiler_params=SMALL,
        name="select_blocks",
    )(flags, pops_old, two, one)

    def hops(shift):
        return min(shift % count_y, -shift % count_y)

    def shifted(block, shift):
        if shift % count_y == 0:
            return block
        return lax.ppermute(block, "by", [((k + shift) % count_y, k) for k in range(count_y)])

    def branch(low, high):
        first, second = (high, low) if hops(high) > hops(low) else (low, high)
        return lambda near, far: (shifted(near, second), shifted(far, first))

    pairs = [(low, high) for low in range(count_y) for high in range(low + 1, count_y)]
    near, far = lax.switch(index[0], [branch(*pair) for pair in pairs], near, far)

    state, first, second = pl.pallas_call(
        collide_kernel,
        out_shape=[shape_of(CHANNELS * EDGE, LANES)] + [shape_of(GROUPS * EDGE, LANES)] * 2,
        in_specs=[VMEM] * 4,
        out_specs=[VMEM] * 3,
        compiler_params=SMALL,
        name="collide_first",
    )(extra, flags, near, far)
    second = lax.ppermute(second, "by", upper)
    first = lax.ppermute(first, "by", lower)
    wide, one, two = pl.pallas_call(
        widen_kernel,
        out_shape=[shape_of(2 * CHANNELS * SPAN, LANES)] + [shape_of(2 * SLOTS, LANES)] * 2,
        in_specs=[VMEM] * 3,
        out_specs=[VMEM] * 3,
        compiler_params=SMALL,
        name="widen_pack",
    )(state, second, first)
    two = lax.ppermute(two, "bx", around)
    one = lax.ppermute(one, "bx", inside)
    rows = pl.pallas_call(
        finish_kernel,
        out_shape=shape_of(POPS * TILES * depth, LANES),
        in_specs=[VMEM] * 3,
        out_specs=VMEM,
        scratch_shapes=[
            pltpu.VMEM((2 * CHANNELS * SPAN, LANES), jnp.float32),
            pltpu.VMEM((2, POPS * SPAN, LANES), jnp.float32),
        ],
        compiler_params=SMALL,
        name="stream_collide_stream",
    )(wide, two, one)
    return (
        rows.reshape(POPS, TILES, depth, LANES).transpose(2, 0, 1, 3).reshape(depth, POPS, TILES * LANES)
    )


def solution(mesh):
    return jax.shard_map(
        local,
        mesh=mesh,
        in_specs=(P(("bx", "by"), None, None), P(), P(("bx", "by")), P(("bx", "by"), None)),
        out_specs=P(("bx", "by"), None, None),
        check_vma=False,
    )
```

```python
import functools

import jax
import jax.numpy as jnp
import numpy as np
from jax import lax
from jax.experimental import pallas as pl
from jax.experimental.pallas import tpu as pltpu
from jax.sharding import PartitionSpec as P

EDGE = 8
POPS = 19
TILES = 4
LANES = 128
ROWS = POPS * TILES
CHANNELS = POPS + 2
SOLID = POPS
RATE = POPS + 1
SPAN = 16
INWARD = 5
SLOTS = CHANNELS + INWARD
GROUPS = (SLOTS + 7) // 8

VELOCITY = (
    (0, 0, 0), (1, 0, 0), (-1, 0, 0), (0, 1, 0), (0, -1, 0), (0, 0, 1), (0, 0, -1),
    (1, 1, 0), (-1, -1, 0), (1, -1, 0), (-1, 1, 0), (1, 0, 1), (-1, 0, -1), (1, 0, -1),
    (-1, 0, 1), (0, 1, 1), (0, -1, -1), (0, 1, -1), (0, -1, 1),
)
WEIGHTS = (1.0 / 3.0,) + (1.0 / 18.0,) * 6 + (1.0 / 36.0,) * 12
MAGIC_TRT = 0.1875

VMEM = pl.BlockSpec(memory_space=pltpu.VMEM)
SMEM = pl.BlockSpec(memory_space=pltpu.SMEM)
HBM = pl.BlockSpec(memory_space=pltpu.HBM)
SMALL = pltpu.CompilerParams(vmem_limit_bytes=4 * 1024 * 1024)


def roll(value, shift, axis):
    size = value.shape[axis]
    shift = shift % size
    return value if shift == 0 else pltpu.roll(value, shift, axis)


def parity():
    return lax.rem(lax.axis_index("bx"), 2) == 1


def moving(axis, sign):
    return [q for q in range(POPS) if VELOCITY[q][axis] == sign]


def lane_of(shape):
    return lax.broadcasted_iota(jnp.int32, shape, len(shape) - 1)


def pair_index(low, high, count):
    return low * (2 * count - low + 1) // 2 + (high - low)


def collide(pops, rate, solid):
    rho = functools.reduce(jnp.add, pops)
    flux = []
    for axis in range(3):
        plus = functools.reduce(jnp.add, [pops[q] for q in range(POPS) if VELOCITY[q][axis] > 0])
        minus = functools.reduce(jnp.add, [pops[q] for q in range(POPS) if VELOCITY[q][axis] < 0])
        flux.append(plus - minus)
    base = rho - 1.5 * (flux[0] * flux[0] + flux[1] * flux[1] + flux[2] * flux[2])
    rate_odd = 1.0 / (MAGIC_TRT / (1.0 / rate - 0.5) + 0.5)
    relaxed = [None] * POPS
    rest = pops[0] - rate * (pops[0] - WEIGHTS[0] * base)
    relaxed[0] = jnp.where(solid, pops[0], rest)
    for q in range(1, POPS, 2):
        one, two = pops[q], pops[q + 1]
        speed = None
        for axis in range(3):
            if VELOCITY[q][axis] != 0:
                term = flux[axis] if VELOCITY[q][axis] > 0 else -flux[axis]
                speed = term if speed is None else speed + term
        even = rate * (0.5 * (one + two) - WEIGHTS[q] * (base + 4.5 * speed * speed))
        odd = rate_odd * (0.5 * (one - two) - (3.0 * WEIGHTS[q]) * speed)
        relaxed[q] = jnp.where(solid, two, one - even - odd)
        relaxed[q + 1] = jnp.where(solid, one, two - even + odd)
    return relaxed


def gather_kernel(
    count_x, count_y, depth, owner_in, pops_in, rate_in, solid_in,
    one_ref, two_ref, extra_ref, index_ref,
    owner_ref, pops_ref, rate_ref, solid_ref, sems,
):
    owner_copy = pltpu.make_async_copy(owner_in, owner_ref, sems.at[0])
    pops_copy = pltpu.make_async_copy(pops_in, pops_ref, sems.at[1])
    rate_copy = pltpu.make_async_copy(rate_in, rate_ref, sems.at[2])
    solid_copy = pltpu.make_async_copy(solid_in, solid_ref, sems.at[3])
    owner_copy.start()
    pops_copy.start()
    rate_copy.start()
    solid_copy.start()
    owner_copy.wait()
    my_x, my_y = lax.axis_index("bx"), lax.axis_index("by")
    myself = my_x * count_y + my_y
    odd = lax.rem(my_x, 2)
    found, level = {}, {}
    for offset in (-1, 0, 1):
        place = my_x + offset
        inside = (place >= 0) & (place < count_x)
        start = jnp.clip(place, 0, count_x - 1) * (count_y * depth)
        for layer in range(depth):
            shift = lax.rem(owner_ref[start + layer], count_y)
            row = lax.rem(my_y - shift + count_y, count_y)
            hit = (owner_ref[start + row * depth + layer] == myself) & inside
            found[offset, layer] = hit.astype(jnp.int32)
            level[offset, layer] = row * depth + layer
    slots = {}
    before = jnp.int32(0)
    for offset in (-1, 0, 1):
        for layer in range(depth):
            slot = before
            for other in range(depth):
                if other != layer:
                    slot = slot + found[offset, other] * (level[offset, other] < level[offset, layer]).astype(jnp.int32)
            slots[offset, layer] = jnp.minimum(slot, pops_ref.shape[0] - 1)
        for layer in range(depth):
            before = before + found[offset, layer]
    start = my_x * (count_y * depth)
    shift0 = lax.rem(owner_ref[start], count_y)
    shift1 = lax.rem(owner_ref[start + 1], count_y)
    low, high = jnp.minimum(shift0, shift1), jnp.maximum(shift0, shift1)
    index_ref[0] = pair_index(low, high, count_y)
    rate_copy.wait()
    solid_copy.wait()
    narrow = lane_of((1, LANES)) < 64
    for tile in range(TILES):
        flags = jnp.where(solid_ref[:, tile * LANES:(tile + 1) * LANES] == 1, 1.0, 0.0)
        lower, upper = flags[0:1, :], flags[1:2, :]
        extra_ref[pl.ds(2 * tile, 1), :] = jnp.where(narrow, lower, roll(upper, 64, 1))
        extra_ref[pl.ds(2 * tile + 1, 1), :] = jnp.where(narrow, roll(lower, 64, 1), upper)
    extra_ref[pl.ds(EDGE, EDGE), :] = jnp.where(lane_of((EDGE, LANES)) < 64, rate_ref[0], rate_ref[1])
    pops_copy.wait()
    for layer in range(depth):
        left, right = slots[-1, layer], slots[1, layer]
        one = jnp.where(odd == 1, left, right)
        two = jnp.where(odd == 1, right, left)
        for ref, slot in ((one_ref, one), (two_ref, two)):
            for tile in range(TILES):
                ref[pl.ds(layer * ROWS + tile * POPS, POPS), :] = pops_ref[slot, :, tile * LANES:(tile + 1) * LANES]


def flags_kernel(count_y, depth, owner_ref, flags_ref):
    my_x, my_y = lax.axis_index("bx"), lax.axis_index("by")
    owner = owner_ref[...]
    level = lax.broadcasted_iota(jnp.int32, owner.shape, 0) * LANES + lane_of(owner.shape)
    start = my_x * (count_y * depth)
    here = level - start

    def total(mask, value):
        picked = jnp.where(mask, value, 0).astype(jnp.float32)
        return jnp.sum(jnp.sum(picked, axis=0, keepdims=True), axis=1, keepdims=True)

    hops, rows = [], []
    for layer in range(2):
        shift = total(here == layer, lax.rem(owner, count_y))
        hops.append((jnp.minimum(shift, count_y - shift), shift))
        column = (here >= 0) & (here < count_y * depth) & (lax.rem(level, depth) == layer)
        hit = column & (lax.rem(owner, count_y) == my_y)
        source = total(hit, lax.div(owner, count_y) - my_x)
        place = total(hit, level)
        slot = total((owner == my_x * count_y + my_y) & (level.astype(jnp.float32) < place), 1)
        rows.append((source, slot))
    (hops0, shift0), (hops1, shift1) = hops
    swapped = (hops1 > hops0) | ((hops1 == hops0) & (shift1 < shift0))
    values = [jnp.where(swapped, 1.0, 0.0)] + [row[k] for k in range(2) for row in rows]
    for k, value in enumerate(values):
        flags_ref[pl.ds(k, 1), :] = jnp.broadcast_to(value, (1, LANES))


def select_kernel(flags_ref, pops_ref, two_ref, one_ref, near_ref, far_ref):
    flags = [flags_ref[pl.ds(k, 1), :] for k in range(5)]
    swapped = flags[0] > 0.5
    partner = jnp.where(parity(), -1.0, 1.0)
    for tile in range(TILES):
        blocks = []
        for layer in range(2):
            source, slot = flags[1 + layer], flags[3 + layer]
            part = pl.ds(layer * ROWS + tile * POPS, POPS)
            block = jnp.where(source == partner, one_ref[part, :], two_ref[part, :])
            for k in range(pops_ref.shape[0]):
                keep = pops_ref[k, :, tile * LANES:(tile + 1) * LANES]
                block = jnp.where((source == 0.0) & (slot == k), keep, block)
            blocks.append(block)
        far_ref[pl.ds(tile * POPS, POPS), :] = jnp.where(swapped, blocks[1], blocks[0])
        near_ref[pl.ds(tile * POPS, POPS), :] = jnp.where(swapped, blocks[0], blocks[1])


def collide_kernel(extra_ref, flags_ref, near_ref, far_ref, state_ref, down_ref, up_ref):
    swapped = flags_ref[pl.ds(0, 1), :] > 0.5
    wide = lane_of((POPS, LANES)) < 64
    for tile in range(TILES):
        part = pl.ds(tile * POPS, POPS)
        far, near = far_ref[part, :], near_ref[part, :]
        lower = jnp.where(swapped, near, far)
        upper = jnp.where(swapped, far, near)
        state_ref[pl.ds(2 * tile, POPS, stride=EDGE), :] = jnp.where(wide, lower, roll(upper, 64, 1))
        state_ref[pl.ds(2 * tile + 1, POPS, stride=EDGE), :] = jnp.where(wide, roll(lower, 64, 1), upper)
    marks, rate = extra_ref[pl.ds(0, EDGE), :], extra_ref[pl.ds(EDGE, EDGE), :]
    relaxed = collide([state_ref[pl.ds(q * EDGE, EDGE), :] for q in range(POPS)], rate, marks > 0.5)
    values = relaxed + [marks, rate]
    for channel, value in enumerate(values):
        state_ref[pl.ds(channel * EDGE, EDGE), :] = value
    part = lane_of((EDGE, LANES)) // 8
    for ref, beside, second, sign in ((down_ref, 0, 1, -1), (up_ref, EDGE - 1, EDGE - 2, 1)):
        slots = [(channel, beside) for channel in range(CHANNELS)] + [(q, second) for q in moving(1, sign)]
        for group in range(GROUPS):
            packed = None
            for k, (channel, row) in enumerate(slots[8 * group:8 * group + 8]):
                for layer in range(2):
                    moved = roll(values[channel], (2 * k + layer) * 8 - (layer * 64 + row * 8), 1)
                    packed = moved if packed is None else jnp.where(part == 2 * k + layer, moved, packed)
            ref[pl.ds(group * EDGE, EDGE), :] = packed


def widen_kernel(state_ref, below_ref, above_ref, wide_ref, one_ref, two_ref):
    odd = parity()
    part = lane_of((EDGE, LANES)) // 8
    extras = ((below_ref, 3, 2, moving(1, 1)), (above_ref, 12, 13, moving(1, -1)))
    for channel in range(CHANNELS):
        value = state_ref[pl.ds(channel * EDGE, EDGE), :]
        for layer in range(2):
            field = roll(value, 32 - 64 * layer, 1)
            for ref, beside, second, inward in extras:
                slots = [(channel, beside)]
                if channel in inward:
                    slots.append((CHANNELS + inward.index(channel), second))
                for slot, place in slots:
                    group, k = divmod(slot, 8)
                    halo = ref[pl.ds(group * EDGE, EDGE), :]
                    field = jnp.where(part == place, roll(halo, place * 8 - (2 * k + layer) * 8, 1), field)
            wide_ref[pl.ds((layer * CHANNELS + channel) * SPAN + 4, EDGE), :] = field
    for layer in range(2):
        base = layer * CHANNELS * SPAN + 4
        left = wide_ref[pl.ds(base, CHANNELS, stride=SPAN), :]
        right = wide_ref[pl.ds(base + EDGE - 1, CHANNELS, stride=SPAN), :]
        one_ref[pl.ds(layer * SLOTS, CHANNELS), :] = jnp.where(odd, left, right)
        two_ref[pl.ds(layer * SLOTS, CHANNELS), :] = jnp.where(odd, right, left)
        for k, (to_left, to_right) in enumerate(zip(moving(0, -1), moving(0, 1))):
            left = wide_ref[pl.ds(base + to_left * SPAN + 1, 1), :]
            right = wide_ref[pl.ds(base + to_right * SPAN + EDGE - 2, 1), :]
            one_ref[pl.ds(layer * SLOTS + CHANNELS + k, 1), :] = jnp.where(odd, left, right)
            two_ref[pl.ds(layer * SLOTS + CHANNELS + k, 1), :] = jnp.where(odd, right, left)


def stream(fields, depth_place):
    moved = [[None] * POPS for _ in fields]
    for q in range(POPS):
        step_x, step_y, step_z = VELOCITY[q]
        for layer in range(2):
            value = roll(fields[layer][q], 8 * step_y + step_z, 1)
            if step_z != 0:
                outer = roll(fields[1 - layer][q], 8 * step_y - 7 * step_z, 1)
                value = jnp.where(depth_place == (0 if step_z > 0 else 7), outer, value)
            moved[layer][q] = roll(value, step_x, 0)
    return moved


def finish_kernel(wide_ref, two_ref, one_ref, out_ref, halo_ref, last_ref):
    odd = parity()
    place = lane_of((SPAN, LANES)) % 8
    row = lax.broadcasted_iota(jnp.int32, (SPAN, LANES), 0)
    own = (row >= 4) & (row < 4 + EDGE)
    for layer in range(2):
        base = layer * CHANNELS * SPAN
        one, two = one_ref[pl.ds(layer * SLOTS, CHANNELS), :], two_ref[pl.ds(layer * SLOTS, CHANNELS), :]
        halo_ref[pl.ds(base + 3, CHANNELS, stride=SPAN), :] = jnp.where(odd, one, two)
        halo_ref[pl.ds(base + 4 + EDGE, CHANNELS, stride=SPAN), :] = jnp.where(odd, two, one)
        for k, (to_left, to_right) in enumerate(zip(moving(0, -1), moving(0, 1))):
            second = pl.ds(layer * SLOTS + CHANNELS + k, 1)
            one, two = one_ref[second, :], two_ref[second, :]
            halo_ref[pl.ds(base + to_right * SPAN + 2, 1), :] = jnp.where(odd, one, two)
            halo_ref[pl.ds(base + to_left * SPAN + 5 + EDGE, 1), :] = jnp.where(odd, two, one)
    fields = [[None] * CHANNELS for _ in range(2)]
    for layer in range(2):
        for channel in range(CHANNELS):
            part = pl.ds((layer * CHANNELS + channel) * SPAN, SPAN)
            fields[layer][channel] = jnp.where(own, wide_ref[part, :], halo_ref[part, :])
    moved = stream([field[:POPS] for field in fields], place)
    relaxed = [collide(moved[layer], fields[layer][RATE], fields[layer][SOLID] > 0.5) for layer in range(2)]
    final = stream(relaxed, place)
    half = lane_of((POPS, LANES)) < 64
    for layer in range(2):
        for q in range(POPS):
            last_ref[layer, pl.ds(q * SPAN, SPAN), :] = final[layer][q]
        for tile in range(TILES):
            even = last_ref[layer, pl.ds(2 * tile + 4, POPS, stride=SPAN), :]
            odd = last_ref[layer, pl.ds(2 * tile + 5, POPS, stride=SPAN), :]
            out_ref[pl.ds(2 * tile + layer, POPS, stride=2 * TILES), :] = jnp.where(half, roll(even, -32, 1), roll(odd, 32, 1))


def shape_of(*dims, dtype=jnp.float32):
    return jax.ShapeDtypeStruct(dims, dtype)


def local(pops_old, old_owner, relax, solid_mask):
    count_x, count_y = lax.axis_size("bx"), lax.axis_size("by")
    depth = relax.shape[0]
    inside = [pair for k in range(0, count_x, 2) for pair in ((k, k + 1), (k + 1, k))]
    across = [pair for k in range(1, count_x - 1, 2) for pair in ((k, k + 1), (k + 1, k))]
    around = across + [(count_x - 1, 0), (0, count_x - 1)]
    up = [(k, (k + 1) % count_y) for k in range(count_y)]
    down = [(k, (k - 1) % count_y) for k in range(count_y)]

    one, two, extra, index = pl.pallas_call(
        functools.partial(gather_kernel, count_x, count_y, depth),
        out_shape=[shape_of(depth * ROWS, LANES)] * 2
        + [shape_of(2 * EDGE, LANES), shape_of(1, dtype=jnp.int32)],
        in_specs=[HBM] * 4,
        out_specs=[VMEM] * 3 + [SMEM],
        scratch_shapes=[
            pltpu.SMEM(old_owner.shape, jnp.int32),
            pltpu.VMEM(pops_old.shape, jnp.float32),
            pltpu.SMEM(relax.shape, jnp.float32),
            pltpu.VMEM(solid_mask.shape, jnp.int32),
            pltpu.SemaphoreType.DMA((4,)),
        ],
        name="gather_blocks",
    )(old_owner, pops_old, relax, solid_mask)
    two = lax.ppermute(two, "bx", across)
    one = lax.ppermute(one, "bx", inside)
    flags = pl.pallas_call(
        functools.partial(flags_kernel, count_y, depth),
        out_shape=shape_of(EDGE, LANES),
        in_specs=[VMEM],
        out_specs=VMEM,
        compiler_params=SMALL,
        name="flags",
    )(old_owner.reshape(-1, LANES))
    near, far = pl.pallas_call(
        select_kernel,
        out_shape=[shape_of(ROWS, LANES)] * 2,
        in_specs=[VMEM] * 4,
        out_specs=[VMEM] * 2,
        compiler_params=SMALL,
        name="select_blocks",
    )(flags, pops_old, two, one)

    def hops(shift):
        return min(shift % count_y, -shift % count_y)

    def shifted(block, shift):
        if shift % count_y == 0:
            return block
        return lax.ppermute(block, "by", [((k + shift) % count_y, k) for k in range(count_y)])

    def branch(low, high):
        first, second = (high, low) if hops(high) > hops(low) else (low, high)
        return lambda near, far: (shifted(near, second), shifted(far, first))

    pairs = [(low, high) for low in range(count_y) for high in range(low, count_y)]
    near, far = lax.switch(index[0], [branch(*pair) for pair in pairs], near, far)

    state, to_below, to_above = pl.pallas_call(
        collide_kernel,
        out_shape=[shape_of(CHANNELS * EDGE, LANES)] + [shape_of(GROUPS * EDGE, LANES)] * 2,
        in_specs=[VMEM] * 4,
        out_specs=[VMEM] * 3,
        compiler_params=SMALL,
        name="collide_first",
    )(extra, flags, near, far)
    below = lax.ppermute(to_above, "by", up)
    above = lax.ppermute(to_below, "by", down)
    wide, one, two = pl.pallas_call(
        widen_kernel,
        out_shape=[shape_of(2 * CHANNELS * SPAN, LANES)] + [shape_of(2 * SLOTS, LANES)] * 2,
        in_specs=[VMEM] * 3,
        out_specs=[VMEM] * 3,
        compiler_params=SMALL,
        name="widen_pack",
    )(state, below, above)
    two = lax.ppermute(two, "bx", around)
    one = lax.ppermute(one, "bx", inside)
    rows = pl.pallas_call(
        finish_kernel,
        out_shape=shape_of(POPS * TILES * depth, LANES),
        in_specs=[VMEM] * 3,
        out_specs=VMEM,
        scratch_shapes=[
            pltpu.VMEM((2 * CHANNELS * SPAN, LANES), jnp.float32),
            pltpu.VMEM((2, POPS * SPAN, LANES), jnp.float32),
        ],
        compiler_params=SMALL,
        name="stream_collide_stream",
    )(wide, two, one)
    return (
        rows.reshape(POPS, TILES, depth, LANES).transpose(2, 0, 1, 3).reshape(depth, POPS, TILES * LANES)
    )


def solution(mesh):
    return jax.shard_map(
        local,
        mesh=mesh,
        in_specs=(P(("bx", "by"), None, None), P(), P(("bx", "by")), P(("bx", "by"), None)),
        out_specs=P(("bx", "by"), None, None),
        check_vma=False,
    )
```
